256 devices in a mesh: row: 32 (over z_lo, x, core), col: 8 (over z_hi, y).
Axes of the slice: x: 4, y: 4, z: 8 (z_hi: 2, z_lo: 4; z = z_hi * 4 + z_lo), core: 2. Of those that a mesh axis runs over, the one named last changes fastest.
Arguments:
- sequence_stack: bfloat16 [64, 1024, 256], P(None, 'row'), may hold values from -6 to 6
- feature_multiplier: float32 [256], replicated, may hold values from 0.1 to 1.9
- first_factor_map: bfloat16 [256, 32], replicated, may hold values from -0.375 to 0.375
- second_factor_map: bfloat16 [256, 32], replicated, may hold values from -0.375 to 0.375
- emitted_map: bfloat16 [1024, 128], replicated, may hold values from -1.5 to 1.5
- emitted_offset: float32 [128], replicated, may hold values from -3 to 3
- upstream_adjoint: bfloat16 [1024, 1024, 128], P('row', 'col'), may hold values from -0.59765625 to 0.59765625
Outputs:
- pair_update: bfloat16 [1024, 1024, 128], P('row', 'col')
- sequence_stack_adjoint: float32 [64, 1024, 256], P(None, 'row')
- factor_maps_adjoint: float32 [2, 256, 32], replicated
- emitted_map_adjoint: float32 [1024, 128], replicated
- emitted_offset_adjoint: float32 [128], replicated
The draws below stay inside these ranges and needn't reach their ends.
All inputs are finite; a program needn't handle non-finite values.
Results may differ from the reference program's by a relative error of at most 0.0072.
Values may be sent and summed in bfloat16 or wider, within the bound.
A program may use at most 64 MiB of HBM per device.

```python
import math
import jax
import jax.numpy as jnp
from jax import lax

FEATURE_DEPTH = 256
HIDDEN_WIDTH = 32
Z = 128
SEQUENCE_TOTAL = 64
AMINO_TOTAL = 1024


def block_levels(rng, dims, pieces, smallest, high):
    factor_of = 1.0
    for dim, parts in pieces:
        draws = jax.random.uniform(jax.random.fold_in(jax.random.fold_in(rng, 6), dim), (parts,), jnp.float32, smallest / len(pieces), high / len(pieces))
        factor_of = factor_of * jnp.repeat(jnp.exp(draws), dims[dim] // parts).reshape((-1,) + (1,) * (len(dims) - 1 - dim))
    return factor_of


def normal_values(stream_key, extent, width, limit, split=(), held_as=jnp.bfloat16):
    values = width * jax.random.normal(stream_key, extent, jnp.float32)
    if split:
        values = values * block_levels(stream_key, extent, split, -0.22, 0.18)
    return jnp.clip(values, -limit, limit).astype(held_as)


def setup_inputs(seed: int = 0) -> dict:
    keys = jax.random.split(jax.random.key(seed), 8)
    sequence_stack = normal_values(keys[0], (SEQUENCE_TOTAL, AMINO_TOTAL, FEATURE_DEPTH), 1.0, 6.0, ((1, 32),))
    feature_multiplier = jnp.clip(1.0 + 0.18 * jax.random.normal(keys[1], (FEATURE_DEPTH,), jnp.float32), 0.1, 1.9)
    first_factor_map = normal_values(keys[2], (FEATURE_DEPTH, HIDDEN_WIDTH), FEATURE_DEPTH ** -0.5, 0.375)
    second_factor_map = normal_values(keys[3], (FEATURE_DEPTH, HIDDEN_WIDTH), FEATURE_DEPTH ** -0.5, 0.375)
    emitted_map = normal_values(keys[4], (HIDDEN_WIDTH * HIDDEN_WIDTH, Z), 0.25, 1.5)
    emitted_offset = normal_values(keys[5], (Z,), 0.5, 3.0, (), jnp.float32)
    upstream_adjoint = normal_values(keys[6], (AMINO_TOTAL, AMINO_TOTAL, Z), 0.1, 0.59765625, ((0, 32), (1, 8)))
    return dict(sequence_stack=sequence_stack, feature_multiplier=feature_multiplier, first_factor_map=first_factor_map, second_factor_map=second_factor_map, emitted_map=emitted_map, emitted_offset=emitted_offset, upstream_adjoint=upstream_adjoint)


def rescale_features(sequence_stack, feature_multiplier):
    quantity_elements = sequence_stack.astype(jnp.float32)
    average = lax.optimization_barrier(jnp.mean(quantity_elements, -1, keepdims=True))
    centered = quantity_elements - average
    variance = lax.optimization_barrier(jnp.mean(centered * centered, -1, keepdims=True))
    reciprocal_spread = lax.rsqrt(variance + 1e-05)
    spread_estimate = centered * reciprocal_spread
    whitened_features = (spread_estimate * feature_multiplier).astype(jnp.bfloat16)
    return (spread_estimate, reciprocal_spread, whitened_features)

def project(whitened_features, weight_matrix):
    alignment_rows, residue_count, channel_count = whitened_features.shape
    flattened_rows = jnp.dot(whitened_features.reshape(alignment_rows * residue_count, channel_count), weight_matrix, preferred_element_type=jnp.float32)
    return flattened_rows.reshape(alignment_rows, residue_count, weight_matrix.shape[1]).astype(jnp.bfloat16)

def pair_block(left_block, right_columns, emitted_map, emitted_offset, cot_blk):
    alignment_rows, local_rows, channel_count = left_block.shape
    column_count = right_columns.shape[1]
    left_flattened = left_block.reshape(alignment_rows, local_rows * channel_count)
    right_flattened = right_columns.reshape(alignment_rows, column_count * channel_count)
    outer_result = jnp.dot(left_flattened.T, right_flattened, preferred_element_type=jnp.float32) * (1.0 / alignment_rows)
    outer = outer_result.reshape(local_rows, channel_count, column_count, channel_count).transpose(0, 2, 1, 3)
    outer = outer.reshape(local_rows * column_count, channel_count * channel_count).astype(jnp.bfloat16)
    coupling_increment = (jnp.dot(outer, emitted_map, preferred_element_type=jnp.float32) + emitted_offset).astype(jnp.bfloat16)
    cot_rows = cot_blk.reshape(local_rows * column_count, cot_blk.shape[2])
    weight_gradient = jnp.dot(outer.T, cot_rows, preferred_element_type=jnp.float32)
    bias_gradient = lax.optimization_barrier(jnp.sum(cot_rows.astype(jnp.float32), 0))
    d_outer = jnp.dot(cot_rows, emitted_map.T, preferred_element_type=jnp.float32).astype(jnp.bfloat16)
    ordered_layout = d_outer.reshape(local_rows, column_count, channel_count, channel_count).transpose(0, 2, 1, 3)
    ordered_layout = ordered_layout.reshape(local_rows * channel_count, column_count * channel_count)
    first_factor_adjoint = jnp.dot(right_flattened, ordered_layout.T, preferred_element_type=jnp.float32) * (1.0 / alignment_rows)
    second_factor_adjoint = jnp.dot(left_flattened, ordered_layout, preferred_element_type=jnp.float32) * (1.0 / alignment_rows)
    return (coupling_increment.reshape(local_rows, column_count, emitted_map.shape[1]), weight_gradient, bias_gradient, first_factor_adjoint.reshape(alignment_rows, local_rows, channel_count), second_factor_adjoint.reshape(alignment_rows, column_count, channel_count))

def sweep_pairs(left_side, right_columns, emitted_map, emitted_offset, upstream_adjoint, block_rows):
    alignment_rows, residue_count, channel_count = left_side.shape
    column_count = right_columns.shape[1]
    blocks = residue_count // block_rows
    initial_totals = (jnp.zeros(emitted_map.shape, jnp.float32), jnp.zeros((emitted_map.shape[1],), jnp.float32), jnp.zeros((alignment_rows, column_count, channel_count), jnp.float32))

    def advance(totals, block_index):
        offset = block_index * block_rows
        left_block = lax.dynamic_slice_in_dim(left_side, offset, block_rows, 1)
        cot_blk = lax.dynamic_slice_in_dim(upstream_adjoint, offset, block_rows, 0)
        coupling_increment, weight_gradient, bias_gradient, first_factor_adjoint, second_factor_adjoint = pair_block(left_block, right_columns, emitted_map, emitted_offset, cot_blk)
        return ((totals[0] + weight_gradient, totals[1] + bias_gradient, totals[2] + second_factor_adjoint), (coupling_increment, first_factor_adjoint))
    totals, (updates, left_sides) = lax.scan(advance, initial_totals, jnp.arange(blocks, dtype=jnp.int32))
    coupling_increment = updates.reshape(residue_count, column_count, emitted_map.shape[1])
    first_factor_adjoint = left_sides.transpose(1, 0, 2, 3).reshape(alignment_rows, residue_count, channel_count)
    return (coupling_increment, totals[0], totals[1], first_factor_adjoint, totals[2])

def closing_iteration(whitened_features, spread_estimate, reciprocal_spread, feature_multiplier, first_factor_map, second_factor_map, first_factor_adjoint, second_factor_adjoint):
    alignment_rows, residue_count, channel_count = whitened_features.shape
    left_gradient16 = first_factor_adjoint.astype(jnp.bfloat16).reshape(alignment_rows * residue_count, -1)
    right_gradient16 = second_factor_adjoint.astype(jnp.bfloat16).reshape(alignment_rows * residue_count, -1)
    normalized_flattened = whitened_features.reshape(alignment_rows * residue_count, channel_count)
    normalized_gradient = jnp.dot(left_gradient16, first_factor_map.T, preferred_element_type=jnp.float32)
    normalized_gradient = normalized_gradient + jnp.dot(right_gradient16, second_factor_map.T, preferred_element_type=jnp.float32)
    stretched_features = normalized_gradient.reshape(alignment_rows, residue_count, channel_count) * feature_multiplier
    sequence_stack_adjoint = reciprocal_spread * (stretched_features - lax.optimization_barrier(jnp.mean(stretched_features, -1, keepdims=True)) - spread_estimate * lax.optimization_barrier(jnp.mean(stretched_features * spread_estimate, -1, keepdims=True)))
    factor_maps_adjoint = jnp.stack([jnp.dot(normalized_flattened.T, left_gradient16, preferred_element_type=jnp.float32), jnp.dot(normalized_flattened.T, right_gradient16, preferred_element_type=jnp.float32)])
    return (sequence_stack_adjoint, factor_maps_adjoint)

def reference(sequence_stack, feature_multiplier, first_factor_map, second_factor_map, emitted_map, emitted_offset, upstream_adjoint):
    spread_estimate, reciprocal_spread, whitened_features = rescale_features(sequence_stack, feature_multiplier)
    left_side = project(whitened_features, first_factor_map)
    right = project(whitened_features, second_factor_map)
    block_rows = math.gcd(AMINO_TOTAL, 64)
    coupling_increment, emitted_map_adjoint, emitted_offset_adjoint, first_factor_adjoint, second_factor_adjoint = sweep_pairs(left_side, right, emitted_map, emitted_offset, upstream_adjoint, block_rows)
    sequence_stack_adjoint, factor_maps_adjoint = closing_iteration(whitened_features, spread_estimate, reciprocal_spread, feature_multiplier, first_factor_map, second_factor_map, first_factor_adjoint, second_factor_adjoint)
    return (coupling_increment, sequence_stack_adjoint, factor_maps_adjoint, emitted_map_adjoint, emitted_offset_adjoint)
```

```python
import functools

import jax
import jax.numpy as jnp
from jax import lax
from jax.experimental import pallas as pl
from jax.experimental.pallas import tpu as pltpu
from jax.sharding import PartitionSpec as P

MESH = pl.DeviceIdType.MESH
F32 = jnp.float32
BF16 = jnp.bfloat16
NN = (((1,), (0,)), ((), ()))
NT = (((1,), (1,)), ((), ()))
TN = (((0,), (0,)), ((), ()))


def mm(a, b, dims=NN):
    return lax.dot_general(a, b, dims, preferred_element_type=F32)


def low_lanes(shape):
    return lax.broadcasted_iota(jnp.int32, shape, 1) < 64


def normalise(x):
    average = jnp.mean(x, -1, keepdims=True)
    centered = x - average
    variance = jnp.mean(centered * centered, -1, keepdims=True)
    inverse = lax.rsqrt(variance + 1e-05)
    return centered * inverse, inverse


def project_kernel(x_ref, gain_ref, wt_ref, la_ref, lb_ref, lt_ref, rb_ref, left, right):
    gain = gain_ref[...]
    wt = wt_ref[...]
    low = low_lanes((32, 128))
    low16 = low_lanes((16, 128))

    @pl.loop(0, 8)
    def _(b):
        x = x_ref[pl.ds(b * 4, 4)].astype(F32).reshape(256, 256)
        standard, _ = normalise(x)
        normed = (standard * gain).astype(BF16)
        both = mm(wt, normed, NT).astype(BF16).astype(F32)
        for p in range(2):
            tile = both[:, p * 128 : (p + 1) * 128]
            turned = pltpu.roll(tile, 64, 1)
            row = pl.multiple_of(b * 128 + p * 64, 64)
            scaled, scaled_turned = tile[:32] * (1 / 64), turned[:32] * (1 / 64)
            zero = jnp.zeros_like(scaled)
            la_ref[pl.ds(row, 32)] = jnp.where(low, scaled, zero).astype(BF16)
            lb_ref[pl.ds(row, 32)] = jnp.where(low, zero, scaled_turned).astype(BF16)
            la_ref[pl.ds(row + 32, 32)] = jnp.where(low, scaled_turned, zero).astype(BF16)
            lb_ref[pl.ds(row + 32, 32)] = jnp.where(low, zero, scaled).astype(BF16)
            left[pl.ds(row, 32)] = scaled
            left[pl.ds(row + 32, 32)] = scaled_turned
            j = b * 4 + p * 2
            right[j] = jnp.where(low16, tile[32:48], turned[48:64])
            right[j + 1] = jnp.where(low16, turned[32:48], tile[48:64])

    for b in range(8):
        lt_ref[:, b * 128 : (b + 1) * 128] = left[b * 128 : (b + 1) * 128].T[:64].astype(BF16)
    rb_ref[...] = jnp.swapaxes(right[...], 0, 1).astype(BF16)


def project(x, gain, wt):
    return pl.pallas_call(
        project_kernel,
        out_shape=(
            jax.ShapeDtypeStruct((1024, 128), BF16),
            jax.ShapeDtypeStruct((1024, 128), BF16),
            jax.ShapeDtypeStruct((64, 1024), BF16),
            jax.ShapeDtypeStruct((16, 32, 128), BF16),
        ),
        scratch_shapes=[pltpu.VMEM((1024, 128), F32), pltpu.VMEM((32, 16, 128), F32)],
        compiler_params=pltpu.CompilerParams(vmem_limit_bytes=32 << 20),
        name="project",
    )(x, gain, wt)


def place():
    r = lax.axis_index("row")
    return r, lax.axis_index("col"), r // 8, (r // 2) % 4, r % 2


def serving_half(z, x, z0, zh):
    gap = jnp.abs(z - z0)
    other = jnp.where(gap == 3, 1, jnp.where(gap == 2, (z + x) % 2, 0))
    return (zh + other) % 2


def gather_kernel(rb_ref, out_ref, land, send, recv, swap_send, swap_recv, own_sem):
    r, c, z, x, core = place()
    zh, y = c // 4, c % 4
    sibling = r + 1 - 2 * core
    goal = r // 4
    goal_zh = goal // 4
    k = r % 4
    barrier = pltpu.get_barrier_semaphore()

    for m in range(2):
        owner = 4 * c + core + 2 * m
        half = serving_half(z, x, owner // 8, zh)
        for q in range(4):
            col = half * 4 + q

            @pl.when(jnp.logical_not((owner == r) & (col == c)))
            def _():
                pl.semaphore_signal(barrier, inc=1, device_id=(owner, col), device_id_type=MESH)

    pl.semaphore_signal(barrier, inc=1, device_id=(sibling, c), device_id_type=MESH)

    count = jnp.int32(1)
    for chip in range(16):
        dz, dx = chip // 4, chip % 4
        serves = serving_half(dz, dx, z, goal_zh) == zh
        myself = (goal == c) & (dz == z) & (dx == x)
        count = count + jnp.where(serves & jnp.logical_not(myself), 1, 0)
    pl.semaphore_wait(barrier, count)

    mine = rb_ref.at[pl.ds(y * 4, 4)]
    slot = land.at[pl.ds(y * 4, 4), k]

    def to(dz, dx):
        return pltpu.make_async_remote_copy(
            src_ref=mine,
            dst_ref=slot,
            send_sem=send.at[dz * 4 + dx],
            recv_sem=recv.at[(k // 2) * 4 + y],
            device_id=(dz * 8 + dx * 2 + core, goal),
            device_id_type=MESH,
        )

    def serves_chip(dz, dx):
        serves = serving_half(dz, dx, z, goal_zh) == zh
        return serves, (goal == c) & (dz == z) & (dx == x)

    for step in range(16):
        dz, dx = (z + step // 4) % 4, (x + step % 4) % 4
        serves, myself = serves_chip(dz, dx)

        @pl.when(serves & jnp.logical_not(myself))
        def _():
            to(dz, dx).start()

        if step == 0:

            @pl.when(serves & myself)
            def _():
                own = pltpu.make_async_copy(mine, slot, own_sem)
                own.start()
                own.wait()

    for q in range(4):
        for m in range(2):
            owner = 4 * c + core + 2 * m
            half = serving_half(z, x, owner // 8, zh)
            part = land.at[pl.ds(q * 4, 4), core + 2 * m]

            @pl.when(jnp.logical_not((owner == r) & (half * 4 + q == c)))
            def _():
                pltpu.make_async_remote_copy(
                    src_ref=part,
                    dst_ref=part,
                    send_sem=swap_send.at[m * 4 + q],
                    recv_sem=recv.at[m * 4 + q],
                    device_id=(sibling, c),
                    device_id_type=MESH,
                ).wait_recv()

            pltpu.make_async_remote_copy(
                src_ref=part,
                dst_ref=part,
                send_sem=swap_send.at[m * 4 + q],
                recv_sem=swap_recv.at[m * 4 + q],
                device_id=(sibling, c),
                device_id_type=MESH,
            ).start()

    for step in range(16):
        dz, dx = (z + step // 4) % 4, (x + step % 4) % 4
        serves, myself = serves_chip(dz, dx)

        @pl.when(serves & jnp.logical_not(myself))
        def _():
            to(dz, dx).wait_send()

    for q in range(4):
        for m in range(2):
            part = land.at[pl.ds(q * 4, 4), core + 2 * m]
            there = land.at[pl.ds(q * 4, 4), 1 - core + 2 * m]
            pltpu.make_async_remote_copy(
                src_ref=part,
                dst_ref=there,
                send_sem=swap_send.at[m * 4 + q],
                recv_sem=swap_recv.at[m * 4 + q],
                device_id=(sibling, c),
                device_id_type=MESH,
            ).wait()
    out_ref[...] = land[...]


def gather(rb):
    return pl.pallas_call(
        gather_kernel,
        out_shape=jax.ShapeDtypeStruct((16, 4, 32, 128), BF16),
        in_specs=[pl.BlockSpec(memory_space=pltpu.VMEM)],
        out_specs=pl.BlockSpec(memory_space=pltpu.VMEM),
        scratch_shapes=[
            pltpu.VMEM((16, 4, 32, 128), BF16),
            pltpu.SemaphoreType.DMA((16,)),
            pltpu.SemaphoreType.DMA((8,)),
            pltpu.SemaphoreType.DMA((8,)),
            pltpu.SemaphoreType.DMA((8,)),
            pltpu.SemaphoreType.DMA,
        ],
        compiler_params=pltpu.CompilerParams(
            collective_id=0, has_side_effects=True, vmem_limit_bytes=32 << 20
        ),
        name="gather_right",
    )(rb)


def sweep_kernel(
    la_ref, lb_ref, lt_ref, rt_ref, g_ref, wp_ref, wpt_ref, off_ref,
    pu_ref, sb_ref, gl_ref, bias_ref,
    put, ot, dt, gla, glb, grq, gwq,
):
    @pl.loop(0, 4)
    def _(q):
        right = rt_ref[pl.ds(pl.multiple_of(q * 512, 512), 512)]
        wq = wp_ref[pl.ds(pl.multiple_of(q * 256, 256), 256)]
        wqt = wpt_ref[q]

        @pl.loop(0, 4)
        def _(b):
            rows = pl.ds(pl.multiple_of(b * 256, 256), 256)
            lanes = pl.ds(pl.multiple_of(b * 1024, 1024), 1024)
            g = g_ref[pl.ds(pl.multiple_of(b * 1024, 1024), 1024)]
            for e2, l_ref in enumerate((la_ref, lb_ref)):
                o = mm(l_ref[rows], right, NT).astype(BF16)
                for e1 in range(4):
                    for i in range(8):
                        e = e2 * 4 + e1
                        ot[e * 32 : e * 32 + 32, i * 128 : i * 128 + 128] = o[
                            i * 32 : i * 32 + 32, e1 * 128 : e1 * 128 + 128
                        ]
            d = mm(wq, g, NT).astype(BF16)
            for e in range(8):
                for i in range(8):
                    dt[i * 32 : i * 32 + 32, e * 128 : e * 128 + 128] = d[
                        e * 32 : e * 32 + 32, i * 128 : i * 128 + 128
                    ]
            outer = ot[...]
            update = mm(wqt, outer)
            gw = mm(outer, g)
            left0 = mm(dt[:, :512], right)
            left1 = mm(dt[:, 512:], right)
            gr = mm(lt_ref[b], dt[...])

            @pl.when(q == 0)
            def _():
                put[:, lanes] = update
                gla[rows] = left0
                glb[rows] = left1

            @pl.when(q != 0)
            def _():
                put[:, lanes] += update
                gla[rows] += left0
                glb[rows] += left1

            @pl.when(b == 0)
            def _():
                gwq[...] = gw
                grq[...] = gr

            @pl.when(b != 0)
            def _():
                gwq[...] += gw
                grq[...] += gr

        for core in range(2):
            for z in range(4):
                at = core * 128 + z * 32
                sb_ref[core, q, z, 64:96] = gwq[at : at + 32].astype(BF16)
        for e1 in range(4):
            tile = jnp.concatenate(
                [grq[:, e1 * 128 : e1 * 128 + 128], grq[:, 512 + e1 * 128 : 640 + e1 * 128]], axis=0
            )
            turned = tile.T.astype(BF16)
            for k in range(4):
                at = (e1 % 2) * 32
                sb_ref[k % 2, q, (k // 2) * 2 + e1 // 2, at : at + 32] = turned[k * 32 : k * 32 + 32]

    low = low_lanes((32, 128))
    for m in range(16):
        even, odd = slice(m * 64, m * 64 + 32), slice(m * 64 + 32, m * 64 + 64)
        first = gla[even] + pltpu.roll(glb[even], 64, 1)
        second = glb[odd] + pltpu.roll(gla[odd], 64, 1)
        gl_ref[m * 32 : m * 32 + 32] = (jnp.where(low, first, second) * (1 / 64)).astype(BF16)

    bias_ref[...] = jnp.zeros_like(bias_ref)
    offset = off_ref[...]

    @pl.loop(0, 32)
    def _(i):
        at = pl.ds(pl.multiple_of(i * 128, 128), 128)
        pu_ref[at] = (put[:, at].T + offset).astype(BF16)
        bias_ref[...] += jnp.sum(g_ref[at].astype(F32).reshape(16, 8, 128), 0)


def sweep(la, lb, lt, rt, g, wp, wpt, off):
    return pl.pallas_call(
        sweep_kernel,
        out_shape=(
            jax.ShapeDtypeStruct((4096, 128), BF16),
            jax.ShapeDtypeStruct((2, 4, 4, 96, 128), BF16),
            jax.ShapeDtypeStruct((512, 128), BF16),
            jax.ShapeDtypeStruct((8, 128), F32),
        ),
        scratch_shapes=[
            pltpu.VMEM((128, 4096), F32),
            pltpu.VMEM((256, 1024), BF16),
            pltpu.VMEM((256, 1024), BF16),
            pltpu.VMEM((1024, 128), F32),
            pltpu.VMEM((1024, 128), F32),
            pltpu.VMEM((64, 1024), F32),
            pltpu.VMEM((256, 128), F32),
        ],
        compiler_params=pltpu.CompilerParams(vmem_limit_bytes=48 << 20),
        name="pair_sweep",
    )(la, lb, lt, rt, g, wp, wpt, off)


def copy_to(src, dst, send_sem, recv_sem, device):
    return pltpu.make_async_remote_copy(
        src_ref=src, dst_ref=dst, send_sem=send_sem, recv_sem=recv_sem,
        device_id=device, device_id_type=MESH,
    )


def reduce_kernel(
    sb_ref, gl_ref, fr_ref, fl_ref, w_ref,
    c1, t1, c2, t2, c3, t3, fr, c4, cl, tl, fl,
    s1, r1, s2, r2, s3, r3, s4, r4, s5, r5, s6, r6, s7, r7,
):
    r, c, z, x, core = place()
    sibling = (r + 1 - 2 * core, c)
    k = core + 2 * (z // 2)
    piece = x * 2 + z % 2

    def x_peer(d):
        return z * 8 + ((x + d) % 4) * 2 + core

    def z_peer(d):
        return ((z + d) % 4) * 8 + x * 2 + core

    def source(n):
        kk = r % 4
        return ((kk // 2) * 2 + n % 2) * 8 + (n // 2) * 2 + kk % 2

    barrier = pltpu.get_barrier_semaphore()

    def signal(device):
        pl.semaphore_signal(barrier, inc=1, device_id=device, device_id_type=MESH)

    signal(sibling)
    for d in range(1, 4):
        signal((x_peer(d), c))
        signal((z_peer(d), c))
    for d in range(1, 8):
        signal((r, (c + d) % 8))
    owner = 4 * c + k
    for n in range(8):

        @pl.when(jnp.logical_not((source(n) == r) & (r // 4 == c)))
        def _():
            signal((source(n), r // 4))

    pl.semaphore_wait(barrier, 14 + 8 - jnp.where(owner == r, 1, 0))

    first = []
    for d in (1, 2, 3, 0):
        xx = (x + d) % 4
        cp = copy_to(sb_ref.at[1 - core, xx], c1.at[xx], s1.at[d], r1.at[d], sibling)
        cp.start()
        first.append((d, xx, cp))
    lefts = []
    for d in range(1, 8):
        cc = (c + d) % 8
        cp = copy_to(gl_ref.at[cc], cl.at[d], s5.at[d], r5.at[d], (r, cc))
        cp.start()
        lefts.append(cp)
    second = []
    for d, xx, cp in first:
        cp.wait_recv()
        t1[xx] = (sb_ref[core, xx].astype(F32) + c1[xx].astype(F32)).astype(BF16)
        if d:
            nx = copy_to(t1.at[xx], c2.at[d], s2.at[d], r2.at[d], (x_peer(d), c))
            nx.start()
            second.append(nx)
    for cp in lefts:
        cp.wait_recv()
    total = gl_ref[c].astype(F32)
    for d in range(1, 8):
        total = total + cl[d].astype(F32)
    tl[...] = total.astype(BF16)
    backs = []
    for d in range(1, 8):
        cp = copy_to(tl, fl.at[c], s6.at[d], r6.at[d], (r, (c + d) % 8))
        cp.start()
        backs.append(cp)
    for cp in second:
        cp.wait_recv()
    third = []
    for d in (1, 2, 3, 0):
        zz = (z + d) % 4
        total = t1[x, zz].astype(F32)
        for n in range(1, 4):
            total = total + c2[n, zz].astype(F32)
        t2[zz] = total.astype(BF16)
        if d:
            cp = copy_to(t2.at[zz], c3.at[d], s3.at[d], r3.at[d], (z_peer(d), c))
            cp.start()
            third.append(cp)
    for cp in third:
        cp.wait_recv()
    total = t2[z].astype(F32)
    for n in range(1, 4):
        total = total + c3[n].astype(F32)
    t3[...] = total.astype(BF16)
    c4[c] = t3[64:96]

    def out_right(cc):
        return copy_to(t3.at[0:64], fr.at[piece], s4.at[cc], r4.at[piece], (owner, cc))

    for cc in range(8):

        @pl.when(jnp.logical_not((owner == r) & (c == cc)))
        def _():
            out_right(cc).start()

    @pl.when(owner == r)
    def _():
        fr[piece] = t3[0:64]

    maps = []
    for d in range(1, 8):
        cp = copy_to(t3.at[64:96], c4.at[c], s7.at[d], r7.at[d], (r, (c + d) % 8))
        cp.start()
        maps.append(cp)

    for cp in backs:
        cp.wait_recv()
    fl_ref[...] = fl[...]
    fl_ref[c] = tl[...]
    for cp in maps:
        cp.wait_recv()
    total = c4[0].astype(F32)
    for n in range(1, 8):
        total = total + c4[n].astype(F32)
    w_ref[...] = total.astype(BF16)
    for n in range(8):

        @pl.when(jnp.logical_not((source(n) == r) & (r // 4 == c)))
        def _():
            copy_to(fr.at[n], fr.at[n], s4.at[n], r4.at[n], (owner, c)).wait_recv()

    fr_ref[...] = fr[...]

    for _, _, cp in first:
        cp.wait_send()
    for cp in lefts + second + backs + third + maps:
        cp.wait_send()
    for cc in range(8):

        @pl.when(jnp.logical_not((owner == r) & (c == cc)))
        def _():
            out_right(cc).wait_send()


def reduce_all(sb, gl):
    vm = pl.BlockSpec(memory_space=pltpu.VMEM)
    sems = []
    for n in (4, 4, 4, 8, 8, 8, 8):
        sems += [pltpu.SemaphoreType.DMA((n,)), pltpu.SemaphoreType.DMA((n,))]
    return pl.pallas_call(
        reduce_kernel,
        out_shape=(
            jax.ShapeDtypeStruct((8, 64, 128), BF16),
            jax.ShapeDtypeStruct((8, 64, 128), BF16),
            jax.ShapeDtypeStruct((32, 128), BF16),
        ),
        in_specs=[vm] * 2,
        out_specs=(vm,) * 3,
        scratch_shapes=[
            pltpu.VMEM((4, 4, 96, 128), BF16),
            pltpu.VMEM((4, 4, 96, 128), BF16),
            pltpu.VMEM((4, 4, 96, 128), BF16),
            pltpu.VMEM((4, 96, 128), BF16),
            pltpu.VMEM((4, 96, 128), BF16),
            pltpu.VMEM((96, 128), BF16),
            pltpu.VMEM((8, 64, 128), BF16),
            pltpu.VMEM((8, 32, 128), BF16),
            pltpu.VMEM((8, 64, 128), BF16),
            pltpu.VMEM((64, 128), BF16),
            pltpu.VMEM((8, 64, 128), BF16),
            *sems,
        ],
        compiler_params=pltpu.CompilerParams(
            collective_id=1, has_side_effects=True, vmem_limit_bytes=32 << 20
        ),
        name="reduce_gradients",
    )(sb, gl)


def closing_kernel(x_ref, gain_ref, wt_ref, fl_ref, fr_ref, adj_ref, fac_ref, right, acc):
    right[...] = jnp.swapaxes(fr_ref[...].astype(F32), 0, 1)
    gain = gain_ref[...]
    wt = wt_ref[...]
    low = low_lanes((16, 128))
    acc[...] = jnp.zeros_like(acc)

    @pl.loop(0, 16)
    def _(m):
        x = x_ref[pl.ds(m * 2, 2)].astype(F32).reshape(128, 256)
        standard, inverse = normalise(x)
        normed = (standard * gain).astype(BF16)
        even, odd = right[2 * m], right[2 * m + 1]
        grads = jnp.concatenate(
            [
                fl_ref[pl.ds(pl.multiple_of(m * 32, 32), 32)],
                jnp.where(low, even, pltpu.roll(odd, 64, 1)).astype(BF16),
                jnp.where(low, pltpu.roll(even, 64, 1), odd).astype(BF16),
            ],
            axis=0,
        )
        acc[...] += mm(grads, normed)
        scaled = mm(grads, wt, TN) * gain
        mean = jnp.mean(scaled, -1, keepdims=True)
        along = jnp.mean(scaled * standard, -1, keepdims=True)
        adj = inverse * (scaled - mean - standard * along)
        adj_ref[pl.ds(m * 2, 2)] = adj.reshape(2, 64, 256)

    for n in range(8):
        fac_ref[n, 0:8] = acc[n * 8 : n * 8 + 8, 0:128]
        fac_ref[n, 8:16] = acc[n * 8 : n * 8 + 8, 128:256]


def closing(x, gain, wt, fl, fr):
    return pl.pallas_call(
        closing_kernel,
        out_shape=(
            jax.ShapeDtypeStruct((32, 64, 256), F32),
            jax.ShapeDtypeStruct((8, 16, 128), F32),
        ),
        scratch_shapes=[pltpu.VMEM((32, 16, 128), F32), pltpu.VMEM((64, 256), F32)],
        compiler_params=pltpu.CompilerParams(vmem_limit_bytes=32 << 20),
        name="closing",
    )(x, gain, wt, fl, fr)


def finish_kernel(
    fac_ref, bias_ref, w_ref, out_ref, ob_ref, wout_ref,
    b1, b2, b3, wz, wx, wc, s1, r1, s2, r2, s3, r3, s4, r4, s5, r5, s6, r6,
):
    r, c, z, x, core = place()
    sibling = (r + 1 - 2 * core, c)

    def plane(d):
        return z * 8 + (r + d) % 8

    def x_peer(d):
        return z * 8 + ((x + d) % 4) * 2 + core

    def z_peer(d):
        return ((z + d) % 4) * 8 + x * 2 + core

    barrier = pltpu.get_barrier_semaphore()
    for d in range(1, 8):
        for device in ((plane(d), c), (r, (c + d) % 8)):
            pl.semaphore_signal(barrier, inc=1, device_id=device, device_id_type=MESH)
    for d in range(1, 4):
        pl.semaphore_signal(barrier, inc=1, device_id=(z_peer(d), c), device_id_type=MESH)
    pl.semaphore_wait(barrier, 17)

    waits = []
    me = r % 8
    b1[me, 0:16] = fac_ref[c]
    b1[me, 16:24] = bias_ref[...]
    one = []
    for d in range(1, 8):
        cp = copy_to(b1.at[me], b1.at[me], s1.at[d], r1.at[d], (plane(d), c))
        cp.start()
        one.append(cp)
    wz[z] = w_ref[...]
    wone = []
    for d in range(1, 4):
        cp = copy_to(wz.at[z], wz.at[z], s4.at[d], r4.at[d], (z_peer(d), c))
        cp.start()
        wone.append(cp)
    for cp in one:
        cp.wait_recv()
    total = b1[0]
    for n in range(1, 8):
        total = total + b1[n]
    b2[z] = total
    two = []
    for d in range(1, 4):
        cp = copy_to(b2.at[z], b2.at[z], s2.at[d], r2.at[d], (z_peer(d), c))
        cp.start()
        two.append(cp)
    for cp in wone:
        cp.wait_recv()
    wx[x] = wz[...]
    wtwo = []
    for d in range(1, 4):
        cp = copy_to(wx.at[x], wx.at[x], s5.at[d], r5.at[d], (x_peer(d), c))
        cp.start()
        wtwo.append(cp)
    for cp in two:
        cp.wait_recv()
    total = b2[0]
    for n in range(1, 4):
        total = total + b2[n]
    b3[c] = total
    three = []
    for d in range(1, 8):
        cp = copy_to(b3.at[c], b3.at[c], s3.at[d], r3.at[d], (r, (c + d) % 8))
        cp.start()
        three.append(cp)
    for cp in wtwo:
        cp.wait_recv()
    wlast = copy_to(wx, wc, s6, r6, sibling)
    wlast.start()
    wout_ref[core] = wx[...]
    for cp in three:
        cp.wait_recv()
    bias = b3[0, 16:24]
    for n in range(1, 8):
        bias = bias + b3[n, 16:24]
    ob_ref[...] = bias
    out_ref[...] = b3[:, 0:16]
    wlast.wait_recv()
    wout_ref[1 - core] = wc[...]
    for cp in one + wone + two + wtwo + three:
        cp.wait_send()
    wlast.wait_send()


def finish(fac, bias, w):
    vm = pl.BlockSpec(memory_space=pltpu.VMEM)
    sems = []
    for n in (8, 4, 8, 4, 4):
        sems += [pltpu.SemaphoreType.DMA((n,)), pltpu.SemaphoreType.DMA((n,))]
    return pl.pallas_call(
        finish_kernel,
        out_shape=(
            jax.ShapeDtypeStruct((8, 16, 128), F32),
            jax.ShapeDtypeStruct((8, 128), F32),
            jax.ShapeDtypeStruct((2, 4, 4, 32, 128), BF16),
        ),
        in_specs=[vm] * 3,
        out_specs=(vm,) * 3,
        scratch_shapes=[
            pltpu.VMEM((8, 24, 128), F32),
            pltpu.VMEM((4, 24, 128), F32),
            pltpu.VMEM((8, 24, 128), F32),
            pltpu.VMEM((4, 32, 128), BF16),
            pltpu.VMEM((4, 4, 32, 128), BF16),
            pltpu.VMEM((4, 4, 32, 128), BF16),
            *sems,
            pltpu.SemaphoreType.DMA,
            pltpu.SemaphoreType.DMA,
        ],
        compiler_params=pltpu.CompilerParams(
            collective_id=2, has_side_effects=True, vmem_limit_bytes=32 << 20
        ),
        name="finish",
    )(fac, bias, w)


def per_device(
    sequence_stack,
    feature_multiplier,
    first_factor_map,
    second_factor_map,
    emitted_map,
    emitted_offset,
    upstream_adjoint,
):
    x = sequence_stack.transpose(1, 0, 2)
    gain = feature_multiplier.reshape(1, 256)
    wt = jnp.concatenate([first_factor_map.T, second_factor_map.T], axis=0)
    wp = emitted_map.reshape(32, 2, 4, 4, 128).transpose(2, 1, 3, 0, 4).reshape(1024, 128)
    wpt = wp.reshape(4, 256, 128).transpose(0, 2, 1)
    g = upstream_adjoint.reshape(4096, 128)

    la, lb, lt, rb = project(x, gain, wt)
    rt = gather(rb).reshape(2048, 128)
    lt = lt.reshape(64, 4, 256).transpose(1, 0, 2)
    pu, sb, gl, bias = sweep(la, lb, lt, rt, g, wp, wpt, emitted_offset.reshape(1, 128))
    fr, fl, w = reduce_all(sb, gl.reshape(8, 64, 128))
    adj, fac = closing(x, gain, wt, fl.reshape(512, 128), fr.reshape(16, 32, 128))
    fac, bias, w = finish(fac, bias, w)
    factor = fac.reshape(8, 2, 8, 128)
    factor = factor.transpose(0, 2, 1, 3).reshape(2, 32, 256).transpose(0, 2, 1)
    map_adjoint = w.reshape(32, 32, 128).transpose(1, 0, 2).reshape(1024, 128).astype(F32)
    return (
        pu.reshape(32, 128, 128),
        adj.transpose(1, 0, 2),
        factor,
        map_adjoint,
        jnp.sum(bias, 0),
    )


def solution(mesh):
    return jax.shard_map(
        per_device,
        mesh=mesh,
        in_specs=(P(None, "row", None), P(), P(), P(), P(), P(), P("row", "col", None)),
        out_specs=(P("row", "col", None), P(None, "row", None), P(), P(), P()),
        check_vma=False,
    )
```

```python
import jax
import jax.numpy as jnp
from jax import lax
from jax.experimental import pallas as pl
from jax.experimental.pallas import tpu as pltpu
from jax.sharding import PartitionSpec as P

MESH = pl.DeviceIdType.MESH
F32 = jnp.float32
BF16 = jnp.bfloat16
NN = (((1,), (0,)), ((), ()))
NT = (((1,), (1,)), ((), ()))
TN = (((0,), (0,)), ((), ()))


def mm(a, b, dims=NN):
    return lax.dot_general(a, b, dims, preferred_element_type=F32)


def low_lanes(shape):
    return lax.broadcasted_iota(jnp.int32, shape, 1) < 64


def normalise(x):
    average = jnp.mean(x, -1, keepdims=True)
    centered = x - average
    variance = jnp.mean(centered * centered, -1, keepdims=True)
    inverse = lax.rsqrt(variance + 1e-05)
    return centered * inverse, inverse


def place():
    r = lax.axis_index("row")
    return r, lax.axis_index("col"), r // 8, (r // 2) % 4, r % 2


def serving_half(z, x, z0, zh):
    gap = jnp.abs(z - z0)
    other = jnp.where(gap == 3, 1, jnp.where(gap == 2, (z + x) % 2, 0))
    return (zh + other) % 2


def copy_to(src, dst, send_sem, recv_sem, device):
    return pltpu.make_async_remote_copy(
        src_ref=src,
        dst_ref=dst,
        send_sem=send_sem,
        recv_sem=recv_sem,
        device_id=device,
        device_id_type=MESH,
    )


def unless(condition):
    return pl.when(jnp.logical_not(condition))


def kernel(
    x_ref, gain_ref, wt_ref, g_ref, wp_ref, wpt_ref, off_ref,
    pu_ref, adj_ref, fac_ref, bias_ref, map_ref,
    la, lb, lt, left, right, rb, land, dt, ot, glx,
    sr, cr1, tr1, cr2, tr2, cr3, tr3, fr,
    sw, cw1, tw1, cw2, tw2, cw3, cw4, wz, wx, wc,
    cl, tl, fl, bias, closing, acc, fs, fc1, fx, fz, ff,
    gs, gd, ks, kd, own_sem,
    s1, r1, s2, r2, s3, r3, s4, r4, s5, r5, s6, r6, s7, r7, s8, r8, s9, r9,
    s10, r10, s11, r11, s12, r12, s13, r13, s14, r14, s15, r15, s16, r16,
):
    r, c, z, x, core = place()
    zh, y = c // 4, c % 4
    sibling = (r + 1 - 2 * core, c)
    goal = r // 4
    k = core + 2 * (z // 2)
    owner = 4 * c + k
    piece = x * 2 + z % 2

    def x_row(xx):
        return z * 8 + xx * 2 + core

    def z_row(zz):
        return zz * 8 + x * 2 + core

    def giver(m, q):
        row = 4 * c + core + 2 * m
        return row, serving_half(z, x, row // 8, zh) * 4 + q

    def source(n):
        return (((r % 4) // 2) * 2 + n % 2) * 8 + (n // 2) * 2 + r % 2

    def chip(step):
        dz, dx = (z + step // 4) % 4, (x + step % 4) % 4
        serves = serving_half(dz, dx, z, goal // 4) == zh
        return dz, dx, serves, (goal == c) & (step == 0)

    barrier = pltpu.get_barrier_semaphore()

    def signal(device):
        pl.semaphore_signal(barrier, inc=1, device_id=device, device_id_type=MESH)

    signal(sibling)
    for d in range(1, 4):
        signal((x_row((x + d) % 4), c))
        signal((z_row((z + d) % 4), c))
    for d in range(1, 8):
        signal((r, (c + d) % 8))
    for n in range(8):

        @unless((source(n) == r) & (goal == c))
        def _():
            signal((source(n), goal))

        row, col = giver(n % 2, n // 2)

        @unless((row == r) & (col == c))
        def _():
            signal((row, col))

    gain = gain_ref[...]
    wt = wt_ref[...]
    low32 = low_lanes((32, 128))
    low16 = low_lanes((16, 128))

    @pl.loop(0, 8)
    def _(b):
        xs = x_ref[pl.ds(b * 4, 4)].astype(F32).reshape(256, 256)
        standard, _ = normalise(xs)
        normed = (standard * gain).astype(BF16)
        both = mm(wt, normed, NT).astype(BF16).astype(F32)
        for p in range(2):
            tile = both[:, p * 128 : (p + 1) * 128]
            turned = pltpu.roll(tile, 64, 1)
            row = pl.multiple_of(b * 128 + p * 64, 64)
            scaled, scaled_turned = tile[:32] * (1 / 64), turned[:32] * (1 / 64)
            zero = jnp.zeros_like(scaled)
            la[pl.ds(row, 32)] = jnp.where(low32, scaled, zero).astype(BF16)
            lb[pl.ds(row, 32)] = jnp.where(low32, zero, scaled_turned).astype(BF16)
            la[pl.ds(row + 32, 32)] = jnp.where(low32, scaled_turned, zero).astype(BF16)
            lb[pl.ds(row + 32, 32)] = jnp.where(low32, zero, scaled).astype(BF16)
            left[pl.ds(row, 32)] = scaled
            left[pl.ds(row + 32, 32)] = scaled_turned
            j = b * 4 + p * 2
            right[j] = jnp.where(low16, tile[32:48], turned[48:64])
            right[j + 1] = jnp.where(low16, turned[32:48], tile[48:64])

    rb[...] = jnp.swapaxes(right[...], 0, 1).astype(BF16)

    count = jnp.int32(14 + 8) - jnp.where(owner == r, 1, 0)
    for step in range(16):
        dz, dx, serves, myself = chip(step)
        count = count + jnp.where(serves & jnp.logical_not(myself), 1, 0)
    pl.semaphore_wait(barrier, count)

    mine = rb.at[pl.ds(y * 4, 4)]
    slot = land.at[pl.ds(y * 4, 4), r % 4]

    def give(step):
        dz, dx, serves, myself = chip(step)
        cp = copy_to(
            mine, slot, gs.at[step], gd.at[((r % 4) // 2) * 4 + y], (dz * 8 + dx * 2 + core, goal)
        )
        return serves & jnp.logical_not(myself), cp

    for step in range(16):
        sends, cp = give(step)

        @pl.when(sends)
        def _():
            cp.start()

    @pl.when((goal == c) & (chip(0)[2]))
    def _():
        own = pltpu.make_async_copy(mine, slot, own_sem)
        own.start()
        own.wait()

    for b in range(8):
        lt[:, b * 128 : (b + 1) * 128] = left[b * 128 : (b + 1) * 128].T[:64].astype(BF16)

    def core_right(q):
        return copy_to(sr.at[1 - core, q], cr1.at[q], s1.at[q], r1.at[q], sibling)

    def x_right(q):
        return copy_to(tr1.at[q], cr2.at[x], s2.at[q], r2.at[x], (x_row(q), c))

    def pass_right(q):
        core_right(q).wait_recv()
        tr1[q] = (sr[core, q].astype(F32) + cr1[q].astype(F32)).astype(BF16)

        @pl.when(x != q)
        def _():
            x_right(q).start()

    @pl.loop(0, 4)
    def _(q):
        wq = wp_ref[pl.ds(pl.multiple_of(q * 256, 256), 256)]

        @pl.loop(0, 4)
        def _(b):
            g = g_ref[pl.ds(pl.multiple_of(b * 1024, 1024), 1024)]
            d = mm(wq, g, NT).astype(BF16)
            for e in range(8):
                for i in range(8):
                    dt[
                        pl.ds(pl.multiple_of(b * 256 + i * 32, 32), 32),
                        pl.ds(pl.multiple_of(q * 1024 + e * 128, 128), 128),
                    ] = d[e * 32 : e * 32 + 32, i * 128 : i * 128 + 128]

        gr = mm(lt[...], dt[:, pl.ds(pl.multiple_of(q * 1024, 1024), 1024)])
        for e1 in range(4):
            tile = jnp.concatenate(
                [gr[:, e1 * 128 : e1 * 128 + 128], gr[:, 512 + e1 * 128 : 640 + e1 * 128]], axis=0
            )
            turned = tile.T.astype(BF16)
            for kk in range(4):
                at = (e1 % 2) * 32
                sr[kk % 2, q, (kk // 2) * 2 + e1 // 2, at : at + 32] = turned[kk * 32 : kk * 32 + 32]
        core_right(q).start()

        @pl.when(q > 0)
        def _():
            pass_right(q - 1)

    def swap(q, m):
        there = land.at[pl.ds(q * 4, 4), core + 2 * m]
        return copy_to(there, there, ks.at[m * 4 + q], kd.at[m * 4 + q], sibling)

    for q in range(4):
        for m in range(2):
            row, col = giver(m, q)
            there = land.at[pl.ds(q * 4, 4), core + 2 * m]

            @unless((row == r) & (col == c))
            def _():
                copy_to(there, there, ks.at[m * 4 + q], gd.at[m * 4 + q], sibling).wait_recv()

            swap(q, m).start()
    pass_right(3)
    for q in range(4):
        for m in range(2):
            there = land.at[pl.ds(q * 4, 4), 1 - core + 2 * m]
            copy_to(there, there, ks.at[m * 4 + q], kd.at[m * 4 + q], sibling).wait_recv()

    bias[...] = jnp.zeros_like(bias)

    @pl.loop(0, 4)
    def _(b):
        rows = pl.ds(pl.multiple_of(b * 256, 256), 256)
        first = jnp.zeros((256, 128), F32)
        second = jnp.zeros((256, 128), F32)
        for q in range(4):
            part = land[q * 4 : q * 4 + 4].reshape(512, 128)
            first = first + mm(dt[rows, q * 1024 : q * 1024 + 512], part)
            second = second + mm(dt[rows, q * 1024 + 512 : q * 1024 + 1024], part)
        for m in range(4):
            even, odd = slice(m * 64, m * 64 + 32), slice(m * 64 + 32, m * 64 + 64)
            one = first[even] + pltpu.roll(second[even], 64, 1)
            two = second[odd] + pltpu.roll(first[odd], 64, 1)
            at = (m % 2) * 32
            glx[b * 2 + m // 2, at : at + 32] = (jnp.where(low32, one, two) * (1 / 64)).astype(BF16)
        g = g_ref[pl.ds(pl.multiple_of(b * 1024, 1024), 1024)]
        bias[...] += jnp.sum(g.astype(F32).reshape(64, 16, 128), 0)

    for n in range(8):
        glx[n, 64:80] = bias[...].astype(BF16)
    lefts = []
    for d in range(1, 8):
        cc = (c + d) % 8
        lefts.append(copy_to(glx.at[cc], cl.at[c], s5.at[d], r5.at[d], (r, cc)))
        lefts[-1].start()

    def core_map(q):
        return copy_to(sw.at[1 - core, q], cw1.at[q], s7.at[q], r7.at[q], sibling)

    def x_map(q):
        return copy_to(tw1.at[q], cw2.at[x], s8.at[q], r8.at[x], (x_row(q), c))

    def pass_map(q):
        core_map(q).wait_recv()
        tw1[q] = (sw[core, q].astype(F32) + cw1[q].astype(F32)).astype(BF16)

        @pl.when(x != q)
        def _():
            x_map(q).start()

    def z_right(d):
        zz = (z + d) % 4
        return copy_to(tr2.at[zz], cr3.at[d], s3.at[d], r3.at[d], (z_row(zz), c))

    def out_right(cc):
        return copy_to(tr3, fr.at[piece], s4.at[cc], r4.at[piece], (owner, cc))

    def out_left(d):
        return copy_to(tl, fl.at[c], s6.at[d], r6.at[d], (r, (c + d) % 8))

    @pl.loop(0, 4)
    def _(q):
        part = land[pl.ds(q * 4, 4)].reshape(512, 128)

        @pl.loop(0, 4)
        def _(b):
            rows = pl.ds(pl.multiple_of(b * 256, 256), 256)
            for e2, l in enumerate((la, lb)):
                o = mm(l[rows], part, NT).astype(BF16)
                for e1 in range(4):
                    for i in range(8):
                        ot[
                            pl.ds(pl.multiple_of(q * 256 + (e2 * 4 + e1) * 32, 32), 32),
                            pl.ds(pl.multiple_of(b * 1024 + i * 128, 128), 128),
                        ] = o[i * 32 : i * 32 + 32, e1 * 128 : e1 * 128 + 128]

        gw = mm(ot[pl.ds(pl.multiple_of(q * 256, 256), 256)], g_ref[...])
        for cc in range(2):
            for zz in range(4):
                at = cc * 128 + zz * 32
                sw[cc, q, zz] = gw[at : at + 32].astype(BF16)
        core_map(q).start()

        @pl.when(q > 0)
        def _():
            pass_map(q - 1)

        @pl.when(q == 1)
        def _():
            for d in range(1, 4):
                n = (x + d) % 4
                copy_to(cr2.at[n], cr2.at[n], s2.at[0], r2.at[n], sibling).wait_recv()
            for d in (1, 2, 3, 0):
                zz = (z + d) % 4
                total = tr1[x, zz].astype(F32)
                for n in range(1, 4):
                    total = total + cr2[(x + n) % 4, zz].astype(F32)
                tr2[zz] = total.astype(BF16)
                if d:
                    z_right(d).start()

        @pl.when(q == 2)
        def _():
            for cp in lefts:
                cp.wait_recv()
            cl[c] = glx[c]
            total = cl[0].astype(F32)
            for n in range(1, 8):
                total = total + cl[n].astype(F32)
            tl[...] = total[:64].astype(BF16)
            bias[...] = total[64:]
            for d in range(1, 8):
                out_left(d).start()

        @pl.when(q == 3)
        def _():
            for d in range(1, 4):
                z_right(d).wait_recv()
            total = tr2[z].astype(F32)
            for n in range(1, 4):
                total = total + cr3[n].astype(F32)
            tr3[...] = total.astype(BF16)
            for cc in range(8):

                @unless((owner == r) & (c == cc))
                def _():
                    out_right(cc).start()

            @pl.when(owner == r)
            def _():
                fr[piece] = tr3[...]

    def z_map(d):
        zz = (z + d) % 4
        return copy_to(tw2.at[zz], cw3.at[d], s9.at[d], r9.at[d], (z_row(zz), c))

    def col_map(d):
        return copy_to(cw4.at[c], cw4.at[c], s10.at[d], r10.at[d], (r, (c + d) % 8))

    offset = off_ref[...]

    @pl.loop(0, 4)
    def _(b):
        update = mm(wpt_ref[...], ot[:, pl.ds(pl.multiple_of(b * 1024, 1024), 1024)])
        for i in range(8):
            at = pl.multiple_of(b * 1024 + i * 128, 128)
            pu_ref[pl.ds(at, 128)] = (update[:, i * 128 : i * 128 + 128].T + offset).astype(BF16)

        @pl.when(b == 0)
        def _():
            pass_map(3)

        @pl.when(b == 3)
        def _():
            for d in range(1, 4):
                n = (x + d) % 4
                copy_to(cw2.at[n], cw2.at[n], s8.at[0], r8.at[n], sibling).wait_recv()
            for d in (1, 2, 3, 0):
                zz = (z + d) % 4
                total = tw1[x, zz].astype(F32)
                for n in range(1, 4):
                    total = total + cw2[(x + n) % 4, zz].astype(F32)
                tw2[zz] = total.astype(BF16)
                if d:
                    z_map(d).start()

    for d in range(1, 8):
        out_left(d).wait_recv()
    fl[c] = tl[...]
    for n in range(8):

        @unless((source(n) == r) & (goal == c))
        def _():
            copy_to(fr.at[n], fr.at[n], s4.at[n], r4.at[n], sibling).wait_recv()

    for d in range(1, 4):
        z_map(d).wait_recv()
    total = tw2[z].astype(F32)
    for n in range(1, 4):
        total = total + cw3[n].astype(F32)
    cw4[c] = total.astype(BF16)
    for d in range(1, 8):
        col_map(d).start()

    closing[...] = jnp.swapaxes(fr[...].reshape(16, 32, 128).astype(F32), 0, 1)
    acc[...] = jnp.zeros_like(acc)

    @pl.loop(0, 16)
    def _(m):
        xs = x_ref[pl.ds(m * 2, 2)].astype(F32).reshape(128, 256)
        standard, inverse = normalise(xs)
        normed = (standard * gain).astype(BF16)
        even, odd = closing[2 * m], closing[2 * m + 1]
        grads = jnp.concatenate(
            [
                fl[m // 2, pl.ds(pl.multiple_of((m % 2) * 32, 32), 32)],
                jnp.where(low16, even, pltpu.roll(odd, 64, 1)).astype(BF16),
                jnp.where(low16, pltpu.roll(even, 64, 1), odd).astype(BF16),
            ],
            axis=0,
        )
        acc[...] += mm(grads, normed)
        scaled = mm(grads, wt, TN) * gain
        mean = jnp.mean(scaled, -1, keepdims=True)
        along = jnp.mean(scaled * standard, -1, keepdims=True)
        adj = inverse * (scaled - mean - standard * along)
        adj_ref[pl.ds(m * 2, 2)] = adj.reshape(2, 64, 256)

    for n in range(2):
        for h in range(2):
            at = h * 32
            fs[n, at : at + 32] = acc[n * 32 : n * 32 + 32, h * 128 : h * 128 + 128]
        fs[n, 64:80] = bias[...]
    half = copy_to(fs.at[1 - core], fc1, s11.at[0], r11.at[0], sibling)
    half.start()
    for d in range(1, 8):
        col_map(d).wait_recv()
    total = cw4[0].astype(F32)
    for n in range(1, 8):
        total = total + cw4[n].astype(F32)
    wz[z] = total.astype(BF16)
    zs = [
        copy_to(wz.at[z], wz.at[z], s12.at[d], r12.at[d], (z_row((z + d) % 4), c)) for d in range(1, 4)
    ]
    for cp in zs:
        cp.start()
    half.wait_recv()
    fx[x] = (fs[core] + fc1[...]).astype(BF16)
    fxs = [
        copy_to(fx.at[x], fx.at[x], s13.at[d], r13.at[d], (x_row((x + d) % 4), c)) for d in range(1, 4)
    ]
    for cp in fxs:
        cp.start()
    for cp in zs:
        cp.wait_recv()
    wx[x] = wz[...]
    xs_ = [
        copy_to(wx.at[x], wx.at[x], s14.at[d], r14.at[d], (x_row((x + d) % 4), c)) for d in range(1, 4)
    ]
    for cp in xs_:
        cp.start()
    for cp in fxs:
        cp.wait_recv()
    total = fx[0].astype(F32)
    for n in range(1, 4):
        total = total + fx[n].astype(F32)
    fz[z] = total.astype(BF16)
    fzs = [
        copy_to(fz.at[z], fz.at[z], s15.at[d], r15.at[d], (z_row((z + d) % 4), c)) for d in range(1, 4)
    ]
    for cp in fzs:
        cp.start()
    for cp in xs_:
        cp.wait_recv()
    last = copy_to(wx, wc, s16.at[0], r16.at[0], sibling)
    last.start()
    map_ref[core] = wx[...]
    for cp in fzs:
        cp.wait_recv()
    total = fz[0].astype(F32)
    for n in range(1, 4):
        total = total + fz[n].astype(F32)
    ff[core] = total[:64]
    end = copy_to(ff.at[core], ff.at[core], s11.at[1], r11.at[1], sibling)
    end.start()
    bias_ref[...] = total[64:]
    last.wait_recv()
    map_ref[1 - core] = wc[...]
    end.wait_recv()
    fac_ref[...] = ff[...]

    for step in range(16):
        sends, cp = give(step)

        @pl.when(sends)
        def _():
            cp.wait_send()

    for q in range(4):
        core_right(q).wait_send()
        core_map(q).wait_send()

        @pl.when(x != q)
        def _():
            x_right(q).wait_send()
            x_map(q).wait_send()

        for m in range(2):
            swap(q, m).wait_send()
    for d in range(1, 4):
        z_right(d).wait_send()
        z_map(d).wait_send()
    for d in range(1, 8):
        out_left(d).wait_send()
        col_map(d).wait_send()
    for cc in range(8):

        @unless((owner == r) & (c == cc))
        def _():
            out_right(cc).wait_send()

    for cp in lefts + zs + fxs + xs_ + fzs + [half, last, end]:
        cp.wait_send()


def run(x, gain, wt, g, wp, wpt, off):
    vm = pl.BlockSpec(memory_space=pltpu.VMEM)

    def b16(*shape):
        return pltpu.VMEM(shape, BF16)

    def f32(*shape):
        return pltpu.VMEM(shape, F32)

    sems = []
    for n in (4, 4, 4, 8, 8, 8, 4, 4, 4, 8, 2, 4, 4, 4, 4, 1):
        sems += [pltpu.SemaphoreType.DMA((n,)), pltpu.SemaphoreType.DMA((n,))]
    return pl.pallas_call(
        kernel,
        out_shape=(
            jax.ShapeDtypeStruct((4096, 128), BF16),
            jax.ShapeDtypeStruct((32, 64, 256), F32),
            jax.ShapeDtypeStruct((2, 64, 128), F32),
            jax.ShapeDtypeStruct((16, 128), F32),
            jax.ShapeDtypeStruct((2, 4, 4, 32, 128), BF16),
        ),
        in_specs=[vm] * 7,
        out_specs=(vm,) * 5,
        scratch_shapes=[
            b16(1024, 128), b16(1024, 128), b16(64, 1024), f32(1024, 128), f32(32, 16, 128),
            b16(16, 32, 128), b16(16, 4, 32, 128), b16(1024, 4096), b16(1024, 4096), b16(8, 80, 128),
            b16(2, 4, 4, 64, 128), b16(4, 4, 64, 128), b16(4, 4, 64, 128), b16(4, 4, 64, 128),
            b16(4, 64, 128), b16(4, 64, 128), b16(64, 128), b16(8, 64, 128),
            b16(2, 4, 4, 32, 128), b16(4, 4, 32, 128), b16(4, 4, 32, 128), b16(4, 4, 32, 128),
            b16(4, 32, 128), b16(4, 32, 128), b16(8, 32, 128), b16(4, 32, 128), b16(4, 4, 32, 128),
            b16(4, 4, 32, 128),
            b16(8, 80, 128), b16(64, 128), b16(8, 64, 128), f32(16, 128), f32(32, 16, 128), f32(64, 256),
            f32(2, 80, 128), f32(80, 128), b16(4, 80, 128), b16(4, 80, 128), f32(2, 64, 128),
            pltpu.SemaphoreType.DMA((16,)), pltpu.SemaphoreType.DMA((8,)),
            pltpu.SemaphoreType.DMA((8,)), pltpu.SemaphoreType.DMA((8,)), pltpu.SemaphoreType.DMA,
            *sems,
        ],
        compiler_params=pltpu.CompilerParams(
            collective_id=0, has_side_effects=True, vmem_limit_bytes=56 << 20
        ),
        name="outer_product_mean",
    )(x, gain, wt, g, wp, wpt, off)


def per_device(
    sequence_stack,
    feature_multiplier,
    first_factor_map,
    second_factor_map,
    emitted_map,
    emitted_offset,
    upstream_adjoint,
):
    x = sequence_stack.transpose(1, 0, 2)
    wt = jnp.concatenate([first_factor_map.T, second_factor_map.T], axis=0)
    wp = emitted_map.reshape(32, 2, 4, 4, 128).transpose(2, 1, 3, 0, 4).reshape(1024, 128)
    pu, adj, fac, bias, w = run(
        x,
        feature_multiplier.reshape(1, 256),
        wt,
        upstream_adjoint.reshape(4096, 128),
        wp,
        wp.T,
        emitted_offset.reshape(1, 128),
    )
    factor = fac.reshape(2, 2, 32, 128).transpose(0, 2, 1, 3).reshape(2, 32, 256).transpose(0, 2, 1)
    return (
        pu.reshape(32, 128, 128),
        adj.transpose(1, 0, 2),
        factor,
        w.reshape(32, 32, 128).transpose(1, 0, 2).reshape(1024, 128).astype(F32),
        jnp.sum(bias, 0),
    )


def solution(mesh):
    return jax.shard_map(
        per_device,
        mesh=mesh,
        in_specs=(P(None, "row", None), P(), P(), P(), P(), P(), P("row", "col", None)),
        out_specs=(P("row", "col", None), P(None, "row", None), P(), P(), P()),
        check_vma=False,
    )
```

```python
import jax
import jax.numpy as jnp
from jax import lax
from jax.experimental import pallas as pl
from jax.experimental.pallas import tpu as pltpu
from jax.sharding import PartitionSpec as P

MESH = pl.DeviceIdType.MESH
F32 = jnp.float32
BF16 = jnp.bfloat16
NN = (((1,), (0,)), ((), ()))
NT = (((1,), (1,)), ((), ()))
TN = (((0,), (0,)), ((), ()))


def mm(a, b, dims=NN):
    return lax.dot_general(a, b, dims, preferred_element_type=F32)


def low_lanes(shape):
    return lax.broadcasted_iota(jnp.int32, shape, 1) < 64


def normalise(x):
    average = jnp.mean(x, -1, keepdims=True)
    centered = x - average
    variance = jnp.mean(centered * centered, -1, keepdims=True)
    inverse = lax.rsqrt(variance + 1e-05)
    return centered * inverse, inverse


def place():
    r = lax.axis_index("row")
    return r, lax.axis_index("col"), r // 8, (r // 2) % 4, r % 2


def serving_half(z, x, z0, zh):
    gap = jnp.abs(z - z0)
    other = jnp.where(gap == 3, 1, jnp.where(gap == 2, (z + x) % 2, 0))
    return (zh + other) % 2


def copy_to(src, dst, send_sem, recv_sem, device):
    return pltpu.make_async_remote_copy(
        src_ref=src,
        dst_ref=dst,
        send_sem=send_sem,
        recv_sem=recv_sem,
        device_id=device,
        device_id_type=MESH,
    )


def unless(condition):
    return pl.when(jnp.logical_not(condition))


def kernel(
    x_ref, gain_ref, w1_ref, w2_ref, g_hbm, w_ref, off_ref,
    pu_hbm, adj_hbm, fac_ref, bias_ref, map_ref,
    st, inv, g_ref, wt_ref, wp_ref, wpt_ref, pu_ref, turn, adj_ref,
    la, lb, lt, left, right, rb, land, dt, ot, glx,
    sr, cr1, tr1, cr2, tr2, cr3, tr3, fr,
    sw, cw1, tw1, cw2, tw2, cw3, cw4, wz, wx, wc,
    cl, tl, fl, bias, closing, acc, grads_all, tall, fs, fc1, fx, fz, ff,
    gs, gd, ks, kd, own_sem, g_sem, pu_sem, adj_sem,
    s1, r1, s2, r2, s3, r3, s4, r4, s5, r5, s6, r6, s7, r7, s8, r8, s9, r9,
    s10, r10, s11, r11, s12, r12, s13, r13, s14, r14, s15, r15, s16, r16,
):
    r, c, z, x, core = place()
    zh, y = c // 4, c % 4
    sibling = (r + 1 - 2 * core, c)
    goal = r // 4
    k = core + 2 * (z // 2)
    owner = 4 * c + k
    piece = x * 2 + z % 2

    def x_row(xx):
        return z * 8 + xx * 2 + core

    def z_row(zz):
        return zz * 8 + x * 2 + core

    def giver(m, q):
        row = 4 * c + core + 2 * m
        return row, serving_half(z, x, row // 8, zh) * 4 + q

    def source(n):
        return (((r % 4) // 2) * 2 + n % 2) * 8 + (n // 2) * 2 + r % 2

    def chip(step):
        dz, dx = (z + step // 4) % 4, (x + step % 4) % 4
        serves = serving_half(dz, dx, z, goal // 4) == zh
        return dz, dx, serves, (goal == c) & (step == 0)

    barrier = pltpu.get_barrier_semaphore()

    def signal(device):
        pl.semaphore_signal(barrier, inc=1, device_id=device, device_id_type=MESH)

    signal(sibling)
    for d in range(1, 4):
        signal((x_row((x + d) % 4), c))
        signal((z_row((z + d) % 4), c))
    for d in range(1, 8):
        signal((r, (c + d) % 8))
    for n in range(8):

        @unless((source(n) == r) & (goal == c))
        def _():
            signal((source(n), goal))

        row, col = giver(n % 2, n // 2)

        @unless((row == r) & (col == c))
        def _():
            signal((row, col))

    bring = pltpu.make_async_copy(g_hbm, g_ref, g_sem)
    bring.start()

    gain = gain_ref[...]
    wt = jnp.concatenate([w1_ref[...], w2_ref[...]], axis=0)
    wt_ref[...] = wt

    @pl.loop(0, 8)
    def _(b):
        rows = pl.ds(pl.multiple_of(b * 8, 8), 8)
        for h in range(2):
            xs = x_ref[rows, h * 16 : h * 16 + 16].astype(F32)
            st[h * 16 : h * 16 + 16, rows] = jnp.swapaxes(xs, 0, 1)

    low32 = low_lanes((32, 128))
    low16 = low_lanes((16, 128))

    @pl.loop(0, 8)
    def _(b):
        standard, inverse = normalise(st[pl.ds(b * 4, 4)].reshape(256, 256))
        st[pl.ds(b * 4, 4)] = standard.reshape(4, 64, 256)
        inv[pl.ds(b * 4, 4)] = inverse.reshape(4, 64, 1)
        normed = (standard * gain).astype(BF16)
        both = mm(wt, normed, NT).astype(BF16).astype(F32)
        for p in range(2):
            tile = both[:, p * 128 : (p + 1) * 128]
            turned = pltpu.roll(tile, 64, 1)
            row = pl.multiple_of(b * 128 + p * 64, 64)
            scaled, scaled_turned = tile[:32] * (1 / 64), turned[:32] * (1 / 64)
            zero = jnp.zeros_like(scaled)
            la[pl.ds(row, 32)] = jnp.where(low32, scaled, zero).astype(BF16)
            lb[pl.ds(row, 32)] = jnp.where(low32, zero, scaled_turned).astype(BF16)
            la[pl.ds(row + 32, 32)] = jnp.where(low32, scaled_turned, zero).astype(BF16)
            lb[pl.ds(row + 32, 32)] = jnp.where(low32, zero, scaled).astype(BF16)
            left[pl.ds(row, 32)] = scaled
            left[pl.ds(row + 32, 32)] = scaled_turned
            j = b * 4 + p * 2
            right[j] = jnp.where(low16, tile[32:48], turned[48:64])
            right[j + 1] = jnp.where(low16, turned[32:48], tile[48:64])

    rb[...] = jnp.swapaxes(right[...], 0, 1).astype(BF16)

    count = jnp.int32(14 + 8) - jnp.where(owner == r, 1, 0)
    for step in range(16):
        dz, dx, serves, myself = chip(step)
        count = count + jnp.where(serves & jnp.logical_not(myself), 1, 0)
    pl.semaphore_wait(barrier, count)

    mine = rb.at[pl.ds(y * 4, 4)]
    slot = land.at[pl.ds(y * 4, 4), r % 4]

    def give(step):
        dz, dx, serves, myself = chip(step)
        cp = copy_to(
            mine, slot, gs.at[step], gd.at[((r % 4) // 2) * 4 + y], (dz * 8 + dx * 2 + core, goal)
        )
        return serves & jnp.logical_not(myself), cp

    for step in range(16):
        sends, cp = give(step)

        @pl.when(sends)
        def _():
            cp.start()

    @pl.when((goal == c) & (chip(0)[2]))
    def _():
        own = pltpu.make_async_copy(mine, slot, own_sem)
        own.start()
        own.wait()

    turn[...] = jnp.swapaxes(w_ref[...].reshape(32, 32, 128).astype(F32), 0, 1)
    for q in range(4):
        for e2 in range(2):
            at = q * 256 + e2 * 128
            tile = turn[e2 * 16 + q * 4 : e2 * 16 + q * 4 + 4].reshape(128, 128)
            wp_ref[at : at + 128] = tile.astype(BF16)
            wpt_ref[:, at : at + 128] = tile.T.astype(BF16)
    for b in range(8):
        lt[:, b * 128 : (b + 1) * 128] = left[b * 128 : (b + 1) * 128].T[:64].astype(BF16)

    bring.wait()

    def core_right(q):
        return copy_to(sr.at[1 - core, q], cr1.at[q], s1.at[q], r1.at[q], sibling)

    def x_right(q):
        return copy_to(tr1.at[q], cr2.at[x], s2.at[q], r2.at[x], (x_row(q), c))

    def pass_right(q):
        core_right(q).wait_recv()
        tr1[q] = (sr[core, q].astype(F32) + cr1[q].astype(F32)).astype(BF16)

        @pl.when(x != q)
        def _():
            x_right(q).start()

    @pl.loop(0, 4)
    def _(q):
        wq = wp_ref[pl.ds(pl.multiple_of(q * 256, 256), 256)]

        @pl.loop(0, 4)
        def _(b):
            g = g_ref[pl.ds(pl.multiple_of(b * 1024, 1024), 1024)]
            d = mm(wq, g, NT).astype(BF16)
            for e in range(8):
                for i in range(8):
                    dt[
                        pl.ds(pl.multiple_of(b * 256 + i * 32, 32), 32),
                        pl.ds(pl.multiple_of(q * 1024 + e * 128, 128), 128),
                    ] = d[e * 32 : e * 32 + 32, i * 128 : i * 128 + 128]

        gr = mm(lt[...], dt[:, pl.ds(pl.multiple_of(q * 1024, 1024), 1024)])
        for e1 in range(4):
            tile = jnp.concatenate(
                [gr[:, e1 * 128 : e1 * 128 + 128], gr[:, 512 + e1 * 128 : 640 + e1 * 128]], axis=0
            )
            turned = tile.T.astype(BF16)
            for kk in range(4):
                at = (e1 % 2) * 32
                sr[kk % 2, q, (kk // 2) * 2 + e1 // 2, at : at + 32] = turned[kk * 32 : kk * 32 + 32]
        core_right(q).start()

        @pl.when(q > 0)
        def _():
            pass_right(q - 1)

    def swap(q, m):
        there = land.at[pl.ds(q * 4, 4), core + 2 * m]
        return copy_to(there, there, ks.at[m * 4 + q], kd.at[m * 4 + q], sibling)

    for q in range(4):
        for m in range(2):
            row, col = giver(m, q)
            there = land.at[pl.ds(q * 4, 4), core + 2 * m]

            @unless((row == r) & (col == c))
            def _():
                copy_to(there, there, ks.at[m * 4 + q], gd.at[m * 4 + q], sibling).wait_recv()

            swap(q, m).start()
    pass_right(3)
    for q in range(4):
        for m in range(2):
            there = land.at[pl.ds(q * 4, 4), 1 - core + 2 * m]
            copy_to(there, there, ks.at[m * 4 + q], kd.at[m * 4 + q], sibling).wait_recv()

    bias[...] = jnp.zeros_like(bias)

    @pl.loop(0, 4)
    def _(b):
        rows = pl.ds(pl.multiple_of(b * 256, 256), 256)
        first = jnp.zeros((256, 128), F32)
        second = jnp.zeros((256, 128), F32)
        for q in range(4):
            part = land[q * 4 : q * 4 + 4].reshape(512, 128)
            first = first + mm(dt[rows, q * 1024 : q * 1024 + 512], part)
            second = second + mm(dt[rows, q * 1024 + 512 : q * 1024 + 1024], part)
        for m in range(4):
            even, odd = slice(m * 64, m * 64 + 32), slice(m * 64 + 32, m * 64 + 64)
            one = first[even] + pltpu.roll(second[even], 64, 1)
            two = second[odd] + pltpu.roll(first[odd], 64, 1)
            at = (m % 2) * 32
            glx[b * 2 + m // 2, at : at + 32] = (jnp.where(low32, one, two) * (1 / 64)).astype(BF16)
        g = g_ref[pl.ds(pl.multiple_of(b * 1024, 1024), 1024)]
        bias[...] += jnp.sum(g.astype(F32).reshape(64, 16, 128), 0)

    for n in range(8):
        glx[n, 64:80] = bias[...].astype(BF16)
    lefts = []
    for d in range(1, 8):
        cc = (c + d) % 8
        lefts.append(copy_to(glx.at[cc], cl.at[c], s5.at[d], r5.at[d], (r, cc)))
        lefts[-1].start()

    def core_map(q):
        return copy_to(sw.at[1 - core, q], cw1.at[q], s7.at[q], r7.at[q], sibling)

    def x_map(q):
        return copy_to(tw1.at[q], cw2.at[x], s8.at[q], r8.at[x], (x_row(q), c))

    def pass_map(q):
        core_map(q).wait_recv()
        tw1[q] = (sw[core, q].astype(F32) + cw1[q].astype(F32)).astype(BF16)

        @pl.when(x != q)
        def _():
            x_map(q).start()

    def z_right(d):
        zz = (z + d) % 4
        return copy_to(tr2.at[zz], cr3.at[d], s3.at[d], r3.at[d], (z_row(zz), c))

    def out_right(cc):
        return copy_to(tr3, fr.at[piece], s4.at[cc], r4.at[piece], (owner, cc))

    def out_left(d):
        return copy_to(tl, fl.at[c], s6.at[d], r6.at[d], (r, (c + d) % 8))

    @pl.loop(0, 4)
    def _(q):
        part = land[pl.ds(q * 4, 4)].reshape(512, 128)

        @pl.loop(0, 4)
        def _(b):
            rows = pl.ds(pl.multiple_of(b * 256, 256), 256)
            for e2, l in enumerate((la, lb)):
                o = mm(l[rows], part, NT).astype(BF16)
                for e1 in range(4):
                    for i in range(8):
                        ot[
                            pl.ds(pl.multiple_of(q * 256 + (e2 * 4 + e1) * 32, 32), 32),
                            pl.ds(pl.multiple_of(b * 1024 + i * 128, 128), 128),
                        ] = o[i * 32 : i * 32 + 32, e1 * 128 : e1 * 128 + 128]

            @pl.when((q == 1) & (b == 0))
            def _():
                for d in range(1, 4):
                    n = (x + d) % 4
                    copy_to(cr2.at[n], cr2.at[n], s2.at[0], r2.at[n], sibling).wait_recv()
                for d in (1, 2, 3, 0):
                    zz = (z + d) % 4
                    total = tr1[x, zz].astype(F32)
                    for n in range(1, 4):
                        total = total + cr2[(x + n) % 4, zz].astype(F32)
                    tr2[zz] = total.astype(BF16)
                    if d:
                        z_right(d).start()

            @pl.when((q == 2) & (b == 3))
            def _():
                for cp in lefts:
                    cp.wait_recv()
                cl[c] = glx[c]
                total = cl[0].astype(F32)
                for n in range(1, 8):
                    total = total + cl[n].astype(F32)
                tl[...] = total[:64].astype(BF16)
                bias[...] = total[64:]
                for d in range(1, 8):
                    out_left(d).start()

            @pl.when((q == 2) & (b == 2))
            def _():
                for d in range(1, 4):
                    z_right(d).wait_recv()
                total = tr2[z].astype(F32)
                for n in range(1, 4):
                    total = total + cr3[n].astype(F32)
                tr3[...] = total.astype(BF16)
                for cc in range(8):

                    @unless((owner == r) & (c == cc))
                    def _():
                        out_right(cc).start()

                @pl.when(owner == r)
                def _():
                    fr[piece] = tr3[...]

        gw = mm(ot[pl.ds(pl.multiple_of(q * 256, 256), 256)], g_ref[...])
        for cc in range(2):
            for zz in range(4):
                at = cc * 128 + zz * 32
                sw[cc, q, zz] = gw[at : at + 32].astype(BF16)
        core_map(q).start()

        @pl.when(q > 0)
        def _():
            pass_map(q - 1)

    def z_map(d):
        zz = (z + d) % 4
        return copy_to(tw2.at[zz], cw3.at[d], s9.at[d], r9.at[d], (z_row(zz), c))

    def col_map(d):
        return copy_to(cw4.at[c], cw4.at[c], s10.at[d], r10.at[d], (r, (c + d) % 8))

    offset = off_ref[...]

    @pl.loop(0, 4)
    def _(b):
        update = mm(wpt_ref[...], ot[:, pl.ds(pl.multiple_of(b * 1024, 1024), 1024)])
        for i in range(8):
            at = pl.multiple_of(b * 1024 + i * 128, 128)
            pu_ref[pl.ds(at, 128)] = (update[:, i * 128 : i * 128 + 128].T + offset).astype(BF16)

        @pl.when(b == 0)
        def _():
            pass_map(3)

    put = pltpu.make_async_copy(pu_ref, pu_hbm, pu_sem)
    put.start()

    for d in range(1, 4):
        n = (x + d) % 4
        copy_to(cw2.at[n], cw2.at[n], s8.at[0], r8.at[n], sibling).wait_recv()
    for d in (1, 2, 3, 0):
        zz = (z + d) % 4
        total = tw1[x, zz].astype(F32)
        for n in range(1, 4):
            total = total + cw2[(x + n) % 4, zz].astype(F32)
        tw2[zz] = total.astype(BF16)
        if d:
            z_map(d).start()

    for d in range(1, 8):
        out_left(d).wait_recv()
    fl[c] = tl[...]
    for n in range(8):

        @unless((source(n) == r) & (goal == c))
        def _():
            copy_to(fr.at[n], fr.at[n], s4.at[n], r4.at[n], sibling).wait_recv()

    closing[...] = jnp.swapaxes(fr[...].reshape(16, 32, 128).astype(F32), 0, 1)

    def pair_grads(m):
        even, odd = closing[2 * m], closing[2 * m + 1]
        return jnp.concatenate(
            [
                fl[m // 2, pl.ds(pl.multiple_of((m % 2) * 32, 32), 32)],
                jnp.where(low16, even, pltpu.roll(odd, 64, 1)).astype(BF16),
                jnp.where(low16, pltpu.roll(even, 64, 1), odd).astype(BF16),
            ],
            axis=0,
        )

    acc[...] = jnp.zeros_like(acc)

    @pl.loop(0, 16)
    def _(m):
        grads = pair_grads(m)
        normed = (st[pl.ds(m * 2, 2)].reshape(128, 256) * gain).astype(BF16)
        acc[...] += mm(grads, normed)
        grads_all[m] = grads

    for n in range(2):
        for h in range(2):
            at = h * 32
            fs[n, at : at + 32] = acc[n * 32 : n * 32 + 32, h * 128 : h * 128 + 128]
        fs[n, 64:80] = bias[...]
    half = copy_to(fs.at[1 - core], fc1, s11.at[0], r11.at[0], sibling)
    half.start()

    def bring_adj(n):
        return pltpu.make_async_copy(
            adj_ref.at[n], adj_hbm.at[:, pl.ds(n * 8, 8)], adj_sem.at[n]
        )

    def adjoint(n):
        @pl.loop(0, 4)
        def _(p):
            m = n * 4 + p
            standard = st[pl.ds(m * 2, 2)].reshape(128, 256)
            inverse = inv[pl.ds(m * 2, 2)].reshape(128, 1)
            scaled = mm(grads_all[m], wt_ref[...], TN) * gain
            mean = jnp.mean(scaled, -1, keepdims=True)
            along = jnp.mean(scaled * standard, -1, keepdims=True)
            adj = inverse * (scaled - mean - standard * along)
            tall[pl.ds(p * 2, 2)] = adj.reshape(2, 64, 256)

        @pl.loop(0, 8)
        def _(b):
            rows = pl.ds(pl.multiple_of(b * 8, 8), 8)
            adj_ref[n, rows] = jnp.swapaxes(tall[:, rows], 0, 1)

        bring_adj(n).start()

    adjoint(0)
    half.wait_recv()
    fx[x] = (fs[core] + fc1[...]).astype(BF16)
    fxs = [
        copy_to(fx.at[x], fx.at[x], s13.at[d], r13.at[d], (x_row((x + d) % 4), c)) for d in range(1, 4)
    ]
    for cp in fxs:
        cp.start()
    adjoint(1)
    for d in range(1, 4):
        z_map(d).wait_recv()
    total = tw2[z].astype(F32)
    for n in range(1, 4):
        total = total + cw3[n].astype(F32)
    cw4[c] = total.astype(BF16)
    for d in range(1, 8):
        col_map(d).start()
    adjoint(2)
    for cp in fxs:
        cp.wait_recv()
    total = fx[0].astype(F32)
    for n in range(1, 4):
        total = total + fx[n].astype(F32)
    fz[z] = total.astype(BF16)
    fzs = [
        copy_to(fz.at[z], fz.at[z], s15.at[d], r15.at[d], (z_row((z + d) % 4), c)) for d in range(1, 4)
    ]
    for cp in fzs:
        cp.start()
    adjoint(3)
    for cp in fzs:
        cp.wait_recv()
    total = fz[0].astype(F32)
    for n in range(1, 4):
        total = total + fz[n].astype(F32)
    ff[core] = total[:64]
    end = copy_to(ff.at[core], ff.at[core], s11.at[1], r11.at[1], sibling)
    end.start()
    bias_ref[...] = jnp.sum(total[64:], 0, keepdims=True)
    for d in range(1, 8):
        col_map(d).wait_recv()
    total = cw4[0].astype(F32)
    for n in range(1, 8):
        total = total + cw4[n].astype(F32)
    wz[z] = total.astype(BF16)
    zs = [
        copy_to(wz.at[z], wz.at[z], s12.at[d], r12.at[d], (z_row((z + d) % 4), c)) for d in range(1, 4)
    ]
    for cp in zs:
        cp.start()
    end.wait_recv()
    for n in range(2):
        for h in range(2):
            fac_ref[n, :, h * 128 : h * 128 + 128] = ff[n, h * 32 : h * 32 + 32]
    for cp in zs:
        cp.wait_recv()
    wx[x] = wz[...]
    xs_ = [
        copy_to(wx.at[x], wx.at[x], s14.at[d], r14.at[d], (x_row((x + d) % 4), c)) for d in range(1, 4)
    ]
    for cp in xs_:
        cp.start()
    for cp in xs_:
        cp.wait_recv()
    last = copy_to(wx, wc, s16.at[0], r16.at[0], sibling)
    last.start()

    def spread(e2, parts):
        map_ref[:, pl.ds(pl.multiple_of(e2 * 16, 16), 16)] = jnp.swapaxes(
            parts.reshape(16, 32, 128).astype(F32), 0, 1
        )

    spread(core, wx[...])
    last.wait_recv()
    spread(1 - core, wc[...])

    for step in range(16):
        sends, cp = give(step)

        @pl.when(sends)
        def _():
            cp.wait_send()

    for q in range(4):
        core_right(q).wait_send()
        core_map(q).wait_send()

        @pl.when(x != q)
        def _():
            x_right(q).wait_send()
            x_map(q).wait_send()

        for m in range(2):
            swap(q, m).wait_send()
    for d in range(1, 4):
        z_right(d).wait_send()
        z_map(d).wait_send()
    for d in range(1, 8):
        out_left(d).wait_send()
        col_map(d).wait_send()
    for cc in range(8):

        @unless((owner == r) & (c == cc))
        def _():
            out_right(cc).wait_send()

    put.wait()
    for n in range(4):
        bring_adj(n).wait()
    for cp in lefts + zs + fxs + xs_ + fzs + [half, last, end]:
        cp.wait_send()


def run(x, gain, w1, w2, g, w, off):
    vm = pl.BlockSpec(memory_space=pltpu.VMEM)
    anywhere = pl.BlockSpec(memory_space=pl.ANY)

    def b16(*shape):
        return pltpu.VMEM(shape, BF16)

    def f32(*shape):
        return pltpu.VMEM(shape, F32)

    sems = []
    for n in (4, 4, 4, 8, 8, 8, 4, 4, 4, 8, 2, 4, 4, 4, 4, 1):
        sems += [pltpu.SemaphoreType.DMA((n,)), pltpu.SemaphoreType.DMA((n,))]
    return pl.pallas_call(
        kernel,
        out_shape=(
            jax.ShapeDtypeStruct((4096, 128), BF16),
            jax.ShapeDtypeStruct((64, 32, 256), F32),
            jax.ShapeDtypeStruct((2, 32, 256), F32),
            jax.ShapeDtypeStruct((1, 128), F32),
            jax.ShapeDtypeStruct((32, 32, 128), F32),
        ),
        in_specs=[vm, vm, vm, vm, anywhere, vm, vm],
        out_specs=(anywhere, anywhere, vm, vm, vm),
        scratch_shapes=[
            f32(32, 64, 256), f32(32, 64, 1), b16(4096, 128), b16(64, 256), b16(1024, 128), b16(128, 1024),
            b16(4096, 128), f32(32, 32, 128), f32(4, 64, 8, 256),
            b16(1024, 128), b16(1024, 128), b16(64, 1024), f32(1024, 128), f32(32, 16, 128),
            b16(16, 32, 128), b16(16, 4, 32, 128), b16(1024, 4096), b16(1024, 4096), b16(8, 80, 128),
            b16(2, 4, 4, 64, 128), b16(4, 4, 64, 128), b16(4, 4, 64, 128), b16(4, 4, 64, 128),
            b16(4, 64, 128), b16(4, 64, 128), b16(64, 128), b16(8, 64, 128),
            b16(2, 4, 4, 32, 128), b16(4, 4, 32, 128), b16(4, 4, 32, 128), b16(4, 4, 32, 128),
            b16(4, 32, 128), b16(4, 32, 128), b16(8, 32, 128), b16(4, 32, 128), b16(4, 4, 32, 128),
            b16(4, 4, 32, 128),
            b16(8, 80, 128), b16(64, 128), b16(8, 64, 128), f32(16, 128), f32(32, 16, 128), f32(64, 256),
            b16(16, 64, 128), f32(8, 64, 256), f32(2, 80, 128), f32(80, 128), b16(4, 80, 128), b16(4, 80, 128), f32(2, 64, 128),
            pltpu.SemaphoreType.DMA((16,)), pltpu.SemaphoreType.DMA((8,)),
            pltpu.SemaphoreType.DMA((8,)), pltpu.SemaphoreType.DMA((8,)), pltpu.SemaphoreType.DMA,
            pltpu.SemaphoreType.DMA, pltpu.SemaphoreType.DMA, pltpu.SemaphoreType.DMA((4,)),
            *sems,
        ],
        compiler_params=pltpu.CompilerParams(
            collective_id=0, has_side_effects=True, vmem_limit_bytes=56 << 20
        ),
        name="outer_product_mean",
    )(x, gain, w1, w2, g, w, off)


def per_device(
    sequence_stack,
    feature_multiplier,
    first_factor_map,
    second_factor_map,
    emitted_map,
    emitted_offset,
    upstream_adjoint,
):
    pu, adj, fac, bias, w = run(
        sequence_stack,
        feature_multiplier.reshape(1, 256),
        first_factor_map.T,
        second_factor_map.T,
        upstream_adjoint.reshape(4096, 128),
        emitted_map,
        emitted_offset.reshape(1, 128),
    )
    return (
        pu.reshape(32, 128, 128),
        adj,
        fac.transpose(0, 2, 1),
        w.reshape(1024, 128),
        bias.reshape(128),
    )


def solution(mesh):
    return jax.shard_map(
        per_device,
        mesh=mesh,
        in_specs=(P(None, "row", None), P(), P(), P(), P(), P(), P("row", "col", None)),
        out_specs=(P("row", "col", None), P(None, "row", None), P(), P(), P()),
        check_vma=False,
    )
```

```python
import jax
import jax.numpy as jnp
from jax import lax
from jax.experimental import pallas as pl
from jax.experimental.pallas import tpu as pltpu
from jax.sharding import PartitionSpec as P

MESH = pl.DeviceIdType.MESH
F32 = jnp.float32
BF16 = jnp.bfloat16
NN = (((1,), (0,)), ((), ()))
NT = (((1,), (1,)), ((), ()))
TN = (((0,), (0,)), ((), ()))


def mm(a, b, dims=NN):
    return lax.dot_general(a, b, dims, preferred_element_type=F32)


def low_lanes(shape):
    return lax.broadcasted_iota(jnp.int32, shape, 1) < 64


def normalise(x):
    average = jnp.mean(x, -1, keepdims=True)
    centered = x - average
    variance = jnp.mean(centered * centered, -1, keepdims=True)
    inverse = lax.rsqrt(variance + 1e-05)
    return centered * inverse, inverse


def place():
    r = lax.axis_index("row")
    return r, lax.axis_index("col"), r // 8, (r // 2) % 4, r % 2


def serving_half(z, x, z0, zh):
    gap = jnp.abs(z - z0)
    other = jnp.where(gap == 3, 1, jnp.where(gap == 2, (z + x) % 2, 0))
    return (zh + other) % 2


def copy_to(src, dst, send_sem, recv_sem, device):
    return pltpu.make_async_remote_copy(
        src_ref=src,
        dst_ref=dst,
        send_sem=send_sem,
        recv_sem=recv_sem,
        device_id=device,
        device_id_type=MESH,
    )


def unless(condition):
    return pl.when(jnp.logical_not(condition))


def kernel(
    x_ref, gain_ref, w1_ref, w2_ref, g_hbm, w_ref, off_ref,
    pu_hbm, adj_hbm, fac_ref, bias_ref, map_ref,
    st, inv, g_ref, wt_ref, wp_ref, wpt_ref, pu_ref, turn, adj_ref,
    la, lb, lt, left, right, rb, land, dt, ot, glx,
    sr, cr1, tr1, cr2, tr2, cr3, tr3, fr,
    sw, cw1, tw1, cw2, tw2, cw3, cw4, wz, wx, wc,
    cl, tl, fl, bias, closing, acc, grads_all, tall, fs, fc1, fx, fz, ff,
    gs, gd, ks, kd, own_sem, g_sem, pu_sem, adj_sem,
    s1, r1, s2, r2, s3, r3, s4, r4, s5, r5, s6, r6, s7, r7, s8, r8, s9, r9,
    s10, r10, s11, r11, s12, r12, s13, r13, s14, r14, s15, r15, s16, r16,
):
    r, c, z, x, core = place()
    zh, y = c // 4, c % 4
    sibling = (r + 1 - 2 * core, c)
    goal = r // 4
    k = core + 2 * (z // 2)
    owner = 4 * c + k
    piece = x * 2 + z % 2

    def x_row(xx):
        return z * 8 + xx * 2 + core

    def z_row(zz):
        return zz * 8 + x * 2 + core

    def giver(m, q):
        row = 4 * c + core + 2 * m
        return row, serving_half(z, x, row // 8, zh) * 4 + q

    def source(n):
        return (((r % 4) // 2) * 2 + n % 2) * 8 + (n // 2) * 2 + r % 2

    def chip(step):
        dz, dx = (z + step // 4) % 4, (x + step % 4) % 4
        serves = serving_half(dz, dx, z, goal // 4) == zh
        return dz, dx, serves, (goal == c) & (step == 0)

    barrier = pltpu.get_barrier_semaphore()

    def signal(device):
        pl.semaphore_signal(barrier, inc=1, device_id=device, device_id_type=MESH)

    signal(sibling)
    for d in range(1, 4):
        signal((x_row((x + d) % 4), c))
        signal((z_row((z + d) % 4), c))
    for d in range(1, 8):
        signal((r, (c + d) % 8))
    for n in range(8):

        @unless((source(n) == r) & (goal == c))
        def _():
            signal((source(n), goal))

        row, col = giver(n % 2, n // 2)

        @unless((row == r) & (col == c))
        def _():
            signal((row, col))

    bring = pltpu.make_async_copy(g_hbm, g_ref, g_sem)
    bring.start()

    gain = gain_ref[...]
    wt = jnp.concatenate([w1_ref[...], w2_ref[...]], axis=0)
    wt_ref[...] = wt

    @pl.loop(0, 8)
    def _(b):
        rows = pl.ds(pl.multiple_of(b * 8, 8), 8)
        for h in range(2):
            xs = x_ref[rows, h * 16 : h * 16 + 16].astype(F32)
            st[h * 16 : h * 16 + 16, rows] = jnp.swapaxes(xs, 0, 1)

    low32 = low_lanes((32, 128))
    low16 = low_lanes((16, 128))

    @pl.loop(0, 8)
    def _(b):
        standard, inverse = normalise(st[pl.ds(b * 4, 4)].reshape(256, 256))
        st[pl.ds(b * 4, 4)] = standard.reshape(4, 64, 256)
        inv[pl.ds(b * 4, 4)] = inverse.reshape(4, 64, 1)
        normed = (standard * gain).astype(BF16)
        both = mm(wt, normed, NT).astype(BF16).astype(F32)
        for p in range(2):
            tile = both[:, p * 128 : (p + 1) * 128]
            turned = pltpu.roll(tile, 64, 1)
            row = pl.multiple_of(b * 128 + p * 64, 64)
            scaled, scaled_turned = tile[:32] * (1 / 64), turned[:32] * (1 / 64)
            zero = jnp.zeros_like(scaled)
            la[pl.ds(row, 32)] = jnp.where(low32, scaled, zero).astype(BF16)
            lb[pl.ds(row, 32)] = jnp.where(low32, zero, scaled_turned).astype(BF16)
            la[pl.ds(row + 32, 32)] = jnp.where(low32, scaled_turned, zero).astype(BF16)
            lb[pl.ds(row + 32, 32)] = jnp.where(low32, zero, scaled).astype(BF16)
            left[pl.ds(row, 32)] = scaled
            left[pl.ds(row + 32, 32)] = scaled_turned
            j = b * 4 + p * 2
            right[j] = jnp.where(low16, tile[32:48], turned[48:64])
            right[j + 1] = jnp.where(low16, turned[32:48], tile[48:64])

    rb[...] = jnp.swapaxes(right[...], 0, 1).astype(BF16)

    count = jnp.int32(14 + 8) - jnp.where(owner == r, 1, 0)
    for step in range(16):
        dz, dx, serves, myself = chip(step)
        count = count + jnp.where(serves & jnp.logical_not(myself), 1, 0)
    pl.semaphore_wait(barrier, count)

    mine = rb.at[pl.ds(y * 4, 4)]
    slot = land.at[pl.ds(y * 4, 4), r % 4]

    def give(step):
        dz, dx, serves, myself = chip(step)
        cp = copy_to(
            mine, slot, gs.at[step], gd.at[((r % 4) // 2) * 4 + y], (dz * 8 + dx * 2 + core, goal)
        )
        return serves & jnp.logical_not(myself), cp

    for step in range(16):
        sends, cp = give(step)

        @pl.when(sends)
        def _():
            cp.start()

    @pl.when((goal == c) & (chip(0)[2]))
    def _():
        own = pltpu.make_async_copy(mine, slot, own_sem)
        own.start()
        own.wait()

    turn[...] = jnp.swapaxes(w_ref[...].reshape(32, 32, 128).astype(F32), 0, 1)
    for q in range(4):
        for e2 in range(2):
            at = q * 256 + e2 * 128
            tile = turn[e2 * 16 + q * 4 : e2 * 16 + q * 4 + 4].reshape(128, 128)
            wp_ref[at : at + 128] = tile.astype(BF16)
            wpt_ref[:, at : at + 128] = tile.T.astype(BF16)
    for b in range(8):
        lt[:, b * 128 : (b + 1) * 128] = left[b * 128 : (b + 1) * 128].T[:64].astype(BF16)

    bring.wait()

    def core_right(q):
        return copy_to(sr.at[1 - core, q], cr1.at[q], s1.at[q], r1.at[q], sibling)

    def x_right(q):
        return copy_to(tr1.at[q], cr2.at[x], s2.at[q], r2.at[x], (x_row(q), c))

    def pass_right(q):
        core_right(q).wait_recv()
        tr1[q] = (sr[core, q].astype(F32) + cr1[q].astype(F32)).astype(BF16)

        @pl.when(x != q)
        def _():
            x_right(q).start()

    @pl.loop(0, 4)
    def _(q):
        wq = wp_ref[pl.ds(pl.multiple_of(q * 256, 256), 256)]

        @pl.loop(0, 2)
        def _(b):
            g = g_ref[pl.ds(pl.multiple_of(b * 2048, 2048), 2048)]
            d = mm(wq, g, NT).astype(BF16)
            for e in range(8):
                for i in range(16):
                    dt[
                        pl.ds(pl.multiple_of(b * 512 + i * 32, 32), 32),
                        pl.ds(pl.multiple_of(q * 1024 + e * 128, 128), 128),
                    ] = d[e * 32 : e * 32 + 32, i * 128 : i * 128 + 128]

        gr = mm(lt[...], dt[:, pl.ds(pl.multiple_of(q * 1024, 1024), 1024)])
        for e1 in range(4):
            tile = jnp.concatenate(
                [gr[:, e1 * 128 : e1 * 128 + 128], gr[:, 512 + e1 * 128 : 640 + e1 * 128]], axis=0
            )
            turned = tile.T.astype(BF16)
            for kk in range(4):
                at = (e1 % 2) * 32
                sr[kk % 2, q, (kk // 2) * 2 + e1 // 2, at : at + 32] = turned[kk * 32 : kk * 32 + 32]
        core_right(q).start()

        @pl.when(q > 0)
        def _():
            pass_right(q - 1)

    def swap(q, m):
        there = land.at[pl.ds(q * 4, 4), core + 2 * m]
        return copy_to(there, there, ks.at[m * 4 + q], kd.at[m * 4 + q], sibling)

    for q in range(4):
        for m in range(2):
            row, col = giver(m, q)
            there = land.at[pl.ds(q * 4, 4), core + 2 * m]

            @unless((row == r) & (col == c))
            def _():
                copy_to(there, there, ks.at[m * 4 + q], gd.at[m * 4 + q], sibling).wait_recv()

            swap(q, m).start()
    pass_right(3)
    for q in range(4):
        for m in range(2):
            there = land.at[pl.ds(q * 4, 4), 1 - core + 2 * m]
            copy_to(there, there, ks.at[m * 4 + q], kd.at[m * 4 + q], sibling).wait_recv()

    bias[...] = jnp.zeros_like(bias)

    @pl.loop(0, 4)
    def _(b):
        rows = pl.ds(pl.multiple_of(b * 256, 256), 256)
        first = jnp.zeros((256, 128), F32)
        second = jnp.zeros((256, 128), F32)
        for q in range(4):
            part = land[q * 4 : q * 4 + 4].reshape(512, 128)
            first = first + mm(dt[rows, q * 1024 : q * 1024 + 512], part)
            second = second + mm(dt[rows, q * 1024 + 512 : q * 1024 + 1024], part)
        for m in range(4):
            even, odd = slice(m * 64, m * 64 + 32), slice(m * 64 + 32, m * 64 + 64)
            one = first[even] + pltpu.roll(second[even], 64, 1)
            two = second[odd] + pltpu.roll(first[odd], 64, 1)
            at = (m % 2) * 32
            glx[b * 2 + m // 2, at : at + 32] = (jnp.where(low32, one, two) * (1 / 64)).astype(BF16)
        g = g_ref[pl.ds(pl.multiple_of(b * 1024, 1024), 1024)]
        bias[...] += jnp.sum(g.astype(F32).reshape(64, 16, 128), 0)

    for n in range(8):
        glx[n, 64:80] = bias[...].astype(BF16)
    lefts = []
    for d in range(1, 8):
        cc = (c + d) % 8
        lefts.append(copy_to(glx.at[cc], cl.at[c], s5.at[d], r5.at[d], (r, cc)))
        lefts[-1].start()

    def core_map(q):
        return copy_to(sw.at[1 - core, q], cw1.at[q], s7.at[q], r7.at[q], sibling)

    def x_map(q):
        return copy_to(tw1.at[q], cw2.at[x], s8.at[q], r8.at[x], (x_row(q), c))

    def pass_map(q):
        core_map(q).wait_recv()
        tw1[q] = (sw[core, q].astype(F32) + cw1[q].astype(F32)).astype(BF16)

        @pl.when(x != q)
        def _():
            x_map(q).start()

    def z_right(d):
        zz = (z + d) % 4
        return copy_to(tr2.at[zz], cr3.at[d], s3.at[d], r3.at[d], (z_row(zz), c))

    def out_right(cc):
        return copy_to(tr3, fr.at[piece], s4.at[cc], r4.at[piece], (owner, cc))

    def out_left(d):
        return copy_to(tl, fl.at[c], s6.at[d], r6.at[d], (r, (c + d) % 8))

    @pl.loop(0, 4)
    def _(q):
        part = land[pl.ds(q * 4, 4)].reshape(512, 128)

        @pl.loop(0, 2)
        def _(b):
            rows = pl.ds(pl.multiple_of(b * 512, 512), 512)
            for e2, l in enumerate((la, lb)):
                o = mm(l[rows], part, NT).astype(BF16)
                for e1 in range(4):
                    for i in range(16):
                        ot[
                            pl.ds(pl.multiple_of(q * 256 + (e2 * 4 + e1) * 32, 32), 32),
                            pl.ds(pl.multiple_of(b * 2048 + i * 128, 128), 128),
                        ] = o[i * 32 : i * 32 + 32, e1 * 128 : e1 * 128 + 128]

            @pl.when((q == 0) & (b == 1))
            def _():
                for d in range(1, 4):
                    n = (x + d) % 4
                    copy_to(cr2.at[n], cr2.at[n], s2.at[0], r2.at[n], sibling).wait_recv()
                for d in (1, 2, 3, 0):
                    zz = (z + d) % 4
                    total = tr1[x, zz].astype(F32)
                    for n in range(1, 4):
                        total = total + cr2[(x + n) % 4, zz].astype(F32)
                    tr2[zz] = total.astype(BF16)
                    if d:
                        z_right(d).start()

            @pl.when((q == 2) & (b == 1))
            def _():
                for cp in lefts:
                    cp.wait_recv()
                cl[c] = glx[c]
                total = cl[0].astype(F32)
                for n in range(1, 8):
                    total = total + cl[n].astype(F32)
                tl[...] = total[:64].astype(BF16)
                bias[...] = total[64:]
                for d in range(1, 8):
                    out_left(d).start()

            @pl.when((q == 1) & (b == 1))
            def _():
                for d in range(1, 4):
                    z_right(d).wait_recv()
                total = tr2[z].astype(F32)
                for n in range(1, 4):
                    total = total + cr3[n].astype(F32)
                tr3[...] = total.astype(BF16)
                for cc in range(8):

                    @unless((owner == r) & (c == cc))
                    def _():
                        out_right(cc).start()

                @pl.when(owner == r)
                def _():
                    fr[piece] = tr3[...]

        gw = mm(ot[pl.ds(pl.multiple_of(q * 256, 256), 256)], g_ref[...])
        for cc in range(2):
            for zz in range(4):
                at = cc * 128 + zz * 32
                sw[cc, q, zz] = gw[at : at + 32].astype(BF16)
        core_map(q).start()

        @pl.when(q > 0)
        def _():
            pass_map(q - 1)

    def z_map(d):
        zz = (z + d) % 4
        return copy_to(tw2.at[zz], cw3.at[d], s9.at[d], r9.at[d], (z_row(zz), c))

    def col_map(d):
        return copy_to(cw4.at[c], cw4.at[c], s10.at[d], r10.at[d], (r, (c + d) % 8))

    offset = off_ref[...]

    @pl.loop(0, 4)
    def _(b):
        update = mm(wpt_ref[...], ot[:, pl.ds(pl.multiple_of(b * 1024, 1024), 1024)])
        for i in range(8):
            at = pl.multiple_of(b * 1024 + i * 128, 128)
            pu_ref[pl.ds(at, 128)] = (update[:, i * 128 : i * 128 + 128].T + offset).astype(BF16)

        @pl.when(b == 0)
        def _():
            pass_map(3)

    put = pltpu.make_async_copy(pu_ref, pu_hbm, pu_sem)
    put.start()

    for d in range(1, 4):
        n = (x + d) % 4
        copy_to(cw2.at[n], cw2.at[n], s8.at[0], r8.at[n], sibling).wait_recv()
    for d in (1, 2, 3, 0):
        zz = (z + d) % 4
        total = tw1[x, zz].astype(F32)
        for n in range(1, 4):
            total = total + cw2[(x + n) % 4, zz].astype(F32)
        tw2[zz] = total.astype(BF16)
        if d:
            z_map(d).start()

    for d in range(1, 8):
        out_left(d).wait_recv()
    fl[c] = tl[...]
    for d in range(1, 4):
        z_map(d).wait_recv()
    total = tw2[z].astype(F32)
    for n in range(1, 4):
        total = total + cw3[n].astype(F32)
    cw4[c] = total.astype(BF16)
    for d in range(1, 8):
        col_map(d).start()
    for n in range(8):

        @unless((source(n) == r) & (goal == c))
        def _():
            copy_to(fr.at[n], fr.at[n], s4.at[n], r4.at[n], sibling).wait_recv()

    closing[...] = jnp.swapaxes(fr[...].reshape(16, 32, 128).astype(F32), 0, 1)

    def pair_grads(m):
        even, odd = closing[2 * m], closing[2 * m + 1]
        return jnp.concatenate(
            [
                fl[m // 2, pl.ds(pl.multiple_of((m % 2) * 32, 32), 32)],
                jnp.where(low16, even, pltpu.roll(odd, 64, 1)).astype(BF16),
                jnp.where(low16, pltpu.roll(even, 64, 1), odd).astype(BF16),
            ],
            axis=0,
        )

    acc[...] = jnp.zeros_like(acc)

    @pl.loop(0, 16)
    def _(m):
        grads = pair_grads(m)
        normed = (st[pl.ds(m * 2, 2)].reshape(128, 256) * gain).astype(BF16)
        acc[...] += mm(grads, normed)
        grads_all[m] = grads

    for n in range(2):
        for h in range(2):
            at = h * 32
            fs[n, at : at + 32] = acc[n * 32 : n * 32 + 32, h * 128 : h * 128 + 128]
        fs[n, 64:80] = bias[...]
    half = copy_to(fs.at[1 - core], fc1, s11.at[0], r11.at[0], sibling)
    half.start()

    def bring_adj(n):
        return pltpu.make_async_copy(
            adj_ref.at[n], adj_hbm.at[:, pl.ds(n * 8, 8)], adj_sem.at[n]
        )

    def adjoint(n):
        @pl.loop(0, 4)
        def _(p):
            m = n * 4 + p
            standard = st[pl.ds(m * 2, 2)].reshape(128, 256)
            inverse = inv[pl.ds(m * 2, 2)].reshape(128, 1)
            scaled = mm(grads_all[m], wt_ref[...], TN) * gain
            mean = jnp.mean(scaled, -1, keepdims=True)
            along = jnp.mean(scaled * standard, -1, keepdims=True)
            adj = inverse * (scaled - mean - standard * along)
            tall[pl.ds(p * 2, 2)] = adj.reshape(2, 64, 256)

        @pl.loop(0, 8)
        def _(b):
            rows = pl.ds(pl.multiple_of(b * 8, 8), 8)
            adj_ref[n, rows] = jnp.swapaxes(tall[:, rows], 0, 1)

        bring_adj(n).start()

    adjoint(0)
    half.wait_recv()
    fx[x] = (fs[core] + fc1[...]).astype(BF16)
    fxs = [
        copy_to(fx.at[x], fx.at[x], s13.at[d], r13.at[d], (x_row((x + d) % 4), c)) for d in range(1, 4)
    ]
    for cp in fxs:
        cp.start()
    adjoint(1)
    adjoint(2)
    for d in range(1, 8):
        col_map(d).wait_recv()
    total = cw4[0].astype(F32)
    for n in range(1, 8):
        total = total + cw4[n].astype(F32)
    wz[z] = total.astype(BF16)
    zs = [
        copy_to(wz.at[z], wz.at[z], s12.at[d], r12.at[d], (z_row((z + d) % 4), c)) for d in range(1, 4)
    ]
    for cp in zs:
        cp.start()
    for cp in fxs:
        cp.wait_recv()
    total = fx[0].astype(F32)
    for n in range(1, 4):
        total = total + fx[n].astype(F32)
    fz[z] = total.astype(BF16)
    fzs = [
        copy_to(fz.at[z], fz.at[z], s15.at[d], r15.at[d], (z_row((z + d) % 4), c)) for d in range(1, 4)
    ]
    for cp in fzs:
        cp.start()
    adjoint(3)
    for cp in zs:
        cp.wait_recv()
    wx[x] = wz[...]
    xs_ = [
        copy_to(wx.at[x], wx.at[x], s14.at[d], r14.at[d], (x_row((x + d) % 4), c)) for d in range(1, 4)
    ]
    for cp in xs_:
        cp.start()
    for cp in fzs:
        cp.wait_recv()
    total = fz[0].astype(F32)
    for n in range(1, 4):
        total = total + fz[n].astype(F32)
    ff[core] = total[:64]
    end = copy_to(ff.at[core], ff.at[core], s11.at[1], r11.at[1], sibling)
    end.start()
    bias_ref[...] = jnp.sum(total[64:], 0, keepdims=True)
    end.wait_recv()
    for n in range(2):
        for h in range(2):
            fac_ref[n, :, h * 128 : h * 128 + 128] = ff[n, h * 32 : h * 32 + 32]
    for cp in xs_:
        cp.wait_recv()
    last = copy_to(wx, wc, s16.at[0], r16.at[0], sibling)
    last.start()

    def spread(e2, parts):
        map_ref[:, pl.ds(pl.multiple_of(e2 * 16, 16), 16)] = jnp.swapaxes(
            parts.reshape(16, 32, 128).astype(F32), 0, 1
        )

    spread(core, wx[...])
    last.wait_recv()
    spread(1 - core, wc[...])

    for step in range(16):
        sends, cp = give(step)

        @pl.when(sends)
        def _():
            cp.wait_send()

    for q in range(4):
        core_right(q).wait_send()
        core_map(q).wait_send()

        @pl.when(x != q)
        def _():
            x_right(q).wait_send()
            x_map(q).wait_send()

        for m in range(2):
            swap(q, m).wait_send()
    for d in range(1, 4):
        z_right(d).wait_send()
        z_map(d).wait_send()
    for d in range(1, 8):
        out_left(d).wait_send()
        col_map(d).wait_send()
    for cc in range(8):

        @unless((owner == r) & (c == cc))
        def _():
            out_right(cc).wait_send()

    put.wait()
    for n in range(4):
        bring_adj(n).wait()
    for cp in lefts + zs + fxs + xs_ + fzs + [half, last, end]:
        cp.wait_send()


def run(x, gain, w1, w2, g, w, off):
    vm = pl.BlockSpec(memory_space=pltpu.VMEM)
    anywhere = pl.BlockSpec(memory_space=pl.ANY)

    def b16(*shape):
        return pltpu.VMEM(shape, BF16)

    def f32(*shape):
        return pltpu.VMEM(shape, F32)

    sems = []
    for n in (4, 4, 4, 8, 8, 8, 4, 4, 4, 8, 2, 4, 4, 4, 4, 1):
        sems += [pltpu.SemaphoreType.DMA((n,)), pltpu.SemaphoreType.DMA((n,))]
    return pl.pallas_call(
        kernel,
        out_shape=(
            jax.ShapeDtypeStruct((4096, 128), BF16),
            jax.ShapeDtypeStruct((64, 32, 256), F32),
            jax.ShapeDtypeStruct((2, 32, 256), F32),
            jax.ShapeDtypeStruct((1, 128), F32),
            jax.ShapeDtypeStruct((32, 32, 128), F32),
        ),
        in_specs=[vm, vm, vm, vm, anywhere, vm, vm],
        out_specs=(anywhere, anywhere, vm, vm, vm),
        scratch_shapes=[
            f32(32, 64, 256), f32(32, 64, 1), b16(4096, 128), b16(64, 256), b16(1024, 128), b16(128, 1024),
            b16(4096, 128), f32(32, 32, 128), f32(4, 64, 8, 256),
            b16(1024, 128), b16(1024, 128), b16(64, 1024), f32(1024, 128), f32(32, 16, 128),
            b16(16, 32, 128), b16(16, 4, 32, 128), b16(1024, 4096), b16(1024, 4096), b16(8, 80, 128),
            b16(2, 4, 4, 64, 128), b16(4, 4, 64, 128), b16(4, 4, 64, 128), b16(4, 4, 64, 128),
            b16(4, 64, 128), b16(4, 64, 128), b16(64, 128), b16(8, 64, 128),
            b16(2, 4, 4, 32, 128), b16(4, 4, 32, 128), b16(4, 4, 32, 128), b16(4, 4, 32, 128),
            b16(4, 32, 128), b16(4, 32, 128), b16(8, 32, 128), b16(4, 32, 128), b16(4, 4, 32, 128),
            b16(4, 4, 32, 128),
            b16(8, 80, 128), b16(64, 128), b16(8, 64, 128), f32(16, 128), f32(32, 16, 128), f32(64, 256),
            b16(16, 64, 128), f32(8, 64, 256), f32(2, 80, 128), f32(80, 128), b16(4, 80, 128), b16(4, 80, 128), f32(2, 64, 128),
            pltpu.SemaphoreType.DMA((16,)), pltpu.SemaphoreType.DMA((8,)),
            pltpu.SemaphoreType.DMA((8,)), pltpu.SemaphoreType.DMA((8,)), pltpu.SemaphoreType.DMA,
            pltpu.SemaphoreType.DMA, pltpu.SemaphoreType.DMA, pltpu.SemaphoreType.DMA((4,)),
            *sems,
        ],
        compiler_params=pltpu.CompilerParams(
            collective_id=0, has_side_effects=True, vmem_limit_bytes=56 << 20
        ),
        name="outer_product_mean",
    )(x, gain, w1, w2, g, w, off)


def per_device(
    sequence_stack,
    feature_multiplier,
    first_factor_map,
    second_factor_map,
    emitted_map,
    emitted_offset,
    upstream_adjoint,
):
    pu, adj, fac, bias, w = run(
        sequence_stack,
        feature_multiplier.reshape(1, 256),
        first_factor_map.T,
        second_factor_map.T,
        upstream_adjoint.reshape(4096, 128),
        emitted_map,
        emitted_offset.reshape(1, 128),
    )
    return (
        pu.reshape(32, 128, 128),
        adj,
        fac.transpose(0, 2, 1),
        w.reshape(1024, 128),
        bias.reshape(128),
    )


def solution(mesh):
    return jax.shard_map(
        per_device,
        mesh=mesh,
        in_specs=(P(None, "row", None), P(), P(), P(), P(), P(), P("row", "col", None)),
        out_specs=(P("row", "col", None), P(None, "row", None), P(), P(), P()),
        check_vma=False,
    )
```

```python
import jax
import jax.numpy as jnp
from jax import lax
from jax.experimental import pallas as pl
from jax.experimental.pallas import tpu as pltpu
from jax.sharding import PartitionSpec as P

MESH = pl.DeviceIdType.MESH
F32 = jnp.float32
BF16 = jnp.bfloat16
NN = (((1,), (0,)), ((), ()))
NT = (((1,), (1,)), ((), ()))
TN = (((0,), (0,)), ((), ()))


def mm(a, b, dims=NN):
    return lax.dot_general(a, b, dims, preferred_element_type=F32)


def low_lanes(shape):
    return lax.broadcasted_iota(jnp.int32, shape, 1) < 64


def normalise(x):
    average = jnp.mean(x, -1, keepdims=True)
    centered = x - average
    variance = jnp.mean(centered * centered, -1, keepdims=True)
    inverse = lax.rsqrt(variance + 1e-05)
    return centered * inverse, inverse


def place():
    r = lax.axis_index("row")
    return r, lax.axis_index("col"), r // 8, (r // 2) % 4, r % 2


def serving_half(z, x, z0, zh):
    gap = jnp.abs(z - z0)
    other = jnp.where(gap == 3, 1, jnp.where(gap == 2, (z + x) % 2, 0))
    return (zh + other) % 2


def copy_to(src, dst, send_sem, recv_sem, device):
    return pltpu.make_async_remote_copy(
        src_ref=src,
        dst_ref=dst,
        send_sem=send_sem,
        recv_sem=recv_sem,
        device_id=device,
        device_id_type=MESH,
    )


def unless(condition):
    return pl.when(jnp.logical_not(condition))


def kernel(
    x_ref, gain_ref, w1_ref, w2_ref, g_hbm, w_ref, off_ref,
    pu_hbm, adj_hbm, fac_ref, bias_ref, map_ref,
    st, inv, g_ref, wt_ref, wp_ref, wpt_ref, pu_ref, turn, adj_ref,
    la, lb, lt, left, right, rb, land, dt, ot, glx,
    sr, cr1, tr1, cr2, tr2, cr3, tr3, fr,
    sw, cw1, tw1, cw2, tw2, cw3, cw4, wz, wx, wc,
    cl, tl, fl, bias, closing, acc, grads_all, tall, fs, fc1, fx, fz, ff,
    gs, gd, ks, kd, own_sem, g_sem, pu_sem, adj_sem,
    s1, r1, s2, r2, s3, r3, s4, r4, s5, r5, s6, r6, s7, r7, s8, r8, s9, r9,
    s10, r10, s11, r11, s12, r12, s13, r13, s14, r14, s15, r15, s16, r16,
):
    r, c, z, x, core = place()
    zh, y = c // 4, c % 4
    sibling = (r + 1 - 2 * core, c)
    goal = r // 4
    k = core + 2 * (z // 2)
    owner = 4 * c + k
    piece = x * 2 + z % 2

    def x_row(xx):
        return z * 8 + xx * 2 + core

    def z_row(zz):
        return zz * 8 + x * 2 + core

    def giver(m, q):
        row = 4 * c + core + 2 * m
        return row, serving_half(z, x, row // 8, zh) * 4 + q

    def source(n):
        return (((r % 4) // 2) * 2 + n % 2) * 8 + (n // 2) * 2 + r % 2

    def chip(step):
        dz, dx = (z + step // 4) % 4, (x + step % 4) % 4
        serves = serving_half(dz, dx, z, goal // 4) == zh
        return dz, dx, serves, (goal == c) & (step == 0)

    barrier = pltpu.get_barrier_semaphore()

    def signal(device):
        pl.semaphore_signal(barrier, inc=1, device_id=device, device_id_type=MESH)

    signal(sibling)
    for d in range(1, 4):
        signal((x_row((x + d) % 4), c))
        signal((z_row((z + d) % 4), c))
    for d in range(1, 8):
        signal((r, (c + d) % 8))
    for n in range(8):

        @unless((source(n) == r) & (goal == c))
        def _():
            signal((source(n), goal))

        row, col = giver(n % 2, n // 2)

        @unless((row == r) & (col == c))
        def _():
            signal((row, col))

    bring = pltpu.make_async_copy(g_hbm, g_ref, g_sem)
    bring.start()

    gain = gain_ref[...]
    wt = jnp.concatenate([w1_ref[...], w2_ref[...]], axis=0)
    wt_ref[...] = wt

    @pl.loop(0, 8, unroll=4)
    def _(b):
        rows = pl.ds(pl.multiple_of(b * 8, 8), 8)
        for h in range(2):
            xs = x_ref[rows, h * 16 : h * 16 + 16].astype(F32)
            st[h * 16 : h * 16 + 16, rows] = jnp.swapaxes(xs, 0, 1)

    low32 = low_lanes((32, 128))
    low16 = low_lanes((16, 128))

    @pl.loop(0, 8, unroll=2)
    def _(b):
        standard, inverse = normalise(st[pl.ds(b * 4, 4)].reshape(256, 256))
        st[pl.ds(b * 4, 4)] = standard.reshape(4, 64, 256)
        inv[pl.ds(b * 4, 4)] = inverse.reshape(4, 64, 1)
        normed = (standard * gain).astype(BF16)
        both = mm(wt, normed, NT).astype(BF16).astype(F32)
        for p in range(2):
            tile = both[:, p * 128 : (p + 1) * 128]
            turned = pltpu.roll(tile, 64, 1)
            row = pl.multiple_of(b * 128 + p * 64, 64)
            scaled, scaled_turned = tile[:32] * (1 / 64), turned[:32] * (1 / 64)
            zero = jnp.zeros_like(scaled)
            la[pl.ds(row, 32)] = jnp.where(low32, scaled, zero).astype(BF16)
            lb[pl.ds(row, 32)] = jnp.where(low32, zero, scaled_turned).astype(BF16)
            la[pl.ds(row + 32, 32)] = jnp.where(low32, scaled_turned, zero).astype(BF16)
            lb[pl.ds(row + 32, 32)] = jnp.where(low32, zero, scaled).astype(BF16)
            left[pl.ds(row, 32)] = scaled
            left[pl.ds(row + 32, 32)] = scaled_turned
            j = b * 4 + p * 2
            right[j] = jnp.where(low16, tile[32:48], turned[48:64])
            right[j + 1] = jnp.where(low16, turned[32:48], tile[48:64])

    rb[...] = jnp.swapaxes(right[...], 0, 1).astype(BF16)

    count = jnp.int32(14 + 8) - jnp.where(owner == r, 1, 0)
    for step in range(16):
        dz, dx, serves, myself = chip(step)
        count = count + jnp.where(serves & jnp.logical_not(myself), 1, 0)
    pl.semaphore_wait(barrier, count)

    mine = rb.at[pl.ds(y * 4, 4)]
    slot = land.at[pl.ds(y * 4, 4), r % 4]

    def give(step):
        dz, dx, serves, myself = chip(step)
        cp = copy_to(
            mine, slot, gs.at[step], gd.at[((r % 4) // 2) * 4 + y], (dz * 8 + dx * 2 + core, goal)
        )
        return serves & jnp.logical_not(myself), cp

    for step in range(16):
        sends, cp = give(step)

        @pl.when(sends)
        def _():
            cp.start()

    @pl.when((goal == c) & (chip(0)[2]))
    def _():
        own = pltpu.make_async_copy(mine, slot, own_sem)
        own.start()
        own.wait()

    turn[...] = jnp.swapaxes(w_ref[...].reshape(32, 32, 128).astype(F32), 0, 1)
    for q in range(4):
        for e2 in range(2):
            at = q * 256 + e2 * 128
            tile = turn[e2 * 16 + q * 4 : e2 * 16 + q * 4 + 4].reshape(128, 128)
            wp_ref[at : at + 128] = tile.astype(BF16)
            wpt_ref[:, at : at + 128] = tile.T.astype(BF16)
    for b in range(8):
        lt[:, b * 128 : (b + 1) * 128] = left[b * 128 : (b + 1) * 128].T[:64].astype(BF16)

    bring.wait()

    def core_right(q):
        return copy_to(sr.at[1 - core, q], cr1.at[q], s1.at[q], r1.at[q], sibling)

    def x_right(q):
        return copy_to(tr1.at[q], cr2.at[x], s2.at[q], r2.at[x], (x_row(q), c))

    def pass_right(q):
        core_right(q).wait_recv()
        tr1[q] = (sr[core, q].astype(F32) + cr1[q].astype(F32)).astype(BF16)

        @pl.when(x != q)
        def _():
            x_right(q).start()

    @pl.loop(0, 4)
    def _(q):
        wq = wp_ref[pl.ds(pl.multiple_of(q * 256, 256), 256)]

        @pl.loop(0, 2, unroll=2)
        def _(b):
            g = g_ref[pl.ds(pl.multiple_of(b * 2048, 2048), 2048)]
            d = mm(wq, g, NT).astype(BF16)
            for e in range(8):
                for i in range(16):
                    dt[
                        pl.ds(pl.multiple_of(b * 512 + i * 32, 32), 32),
                        pl.ds(pl.multiple_of(q * 1024 + e * 128, 128), 128),
                    ] = d[e * 32 : e * 32 + 32, i * 128 : i * 128 + 128]

        gr = mm(lt[...], dt[:, pl.ds(pl.multiple_of(q * 1024, 1024), 1024)])
        for e1 in range(4):
            tile = jnp.concatenate(
                [gr[:, e1 * 128 : e1 * 128 + 128], gr[:, 512 + e1 * 128 : 640 + e1 * 128]], axis=0
            )
            turned = tile.T.astype(BF16)
            for kk in range(4):
                at = (e1 % 2) * 32
                sr[kk % 2, q, (kk // 2) * 2 + e1 // 2, at : at + 32] = turned[kk * 32 : kk * 32 + 32]
        core_right(q).start()

        @pl.when(q > 0)
        def _():
            pass_right(q - 1)

    def swap(q, m):
        there = land.at[pl.ds(q * 4, 4), core + 2 * m]
        return copy_to(there, there, ks.at[m * 4 + q], kd.at[m * 4 + q], sibling)

    for q in range(4):
        for m in range(2):
            row, col = giver(m, q)
            there = land.at[pl.ds(q * 4, 4), core + 2 * m]

            @unless((row == r) & (col == c))
            def _():
                copy_to(there, there, ks.at[m * 4 + q], gd.at[m * 4 + q], sibling).wait_recv()

            swap(q, m).start()
    pass_right(3)
    for q in range(4):
        for m in range(2):
            there = land.at[pl.ds(q * 4, 4), 1 - core + 2 * m]
            copy_to(there, there, ks.at[m * 4 + q], kd.at[m * 4 + q], sibling).wait_recv()

    bias[...] = jnp.zeros_like(bias)

    @pl.loop(0, 4, unroll=2)
    def _(b):
        rows = pl.ds(pl.multiple_of(b * 256, 256), 256)
        first = jnp.zeros((256, 128), F32)
        second = jnp.zeros((256, 128), F32)
        for q in range(4):
            part = land[q * 4 : q * 4 + 4].reshape(512, 128)
            first = first + mm(dt[rows, q * 1024 : q * 1024 + 512], part)
            second = second + mm(dt[rows, q * 1024 + 512 : q * 1024 + 1024], part)
        for m in range(4):
            even, odd = slice(m * 64, m * 64 + 32), slice(m * 64 + 32, m * 64 + 64)
            one = first[even] + pltpu.roll(second[even], 64, 1)
            two = second[odd] + pltpu.roll(first[odd], 64, 1)
            at = (m % 2) * 32
            glx[b * 2 + m // 2, at : at + 32] = (jnp.where(low32, one, two) * (1 / 64)).astype(BF16)
        g = g_ref[pl.ds(pl.multiple_of(b * 1024, 1024), 1024)]
        bias[...] += jnp.sum(g.astype(F32).reshape(64, 16, 128), 0)

    for n in range(8):
        glx[n, 64:80] = bias[...].astype(BF16)
    lefts = []
    for d in range(1, 8):
        cc = (c + d) % 8
        lefts.append(copy_to(glx.at[cc], cl.at[c], s5.at[d], r5.at[d], (r, cc)))
        lefts[-1].start()

    def core_map(q):
        return copy_to(sw.at[1 - core, q], cw1.at[q], s7.at[q], r7.at[q], sibling)

    def x_map(q):
        return copy_to(tw1.at[q], cw2.at[x], s8.at[q], r8.at[x], (x_row(q), c))

    def pass_map(q):
        core_map(q).wait_recv()
        tw1[q] = (sw[core, q].astype(F32) + cw1[q].astype(F32)).astype(BF16)

        @pl.when(x != q)
        def _():
            x_map(q).start()

    def z_right(d):
        zz = (z + d) % 4
        return copy_to(tr2.at[zz], cr3.at[d], s3.at[d], r3.at[d], (z_row(zz), c))

    def out_right(cc):
        return copy_to(tr3, fr.at[piece], s4.at[cc], r4.at[piece], (owner, cc))

    def out_left(d):
        return copy_to(tl, fl.at[c], s6.at[d], r6.at[d], (r, (c + d) % 8))

    @pl.loop(0, 4)
    def _(q):
        part = land[pl.ds(q * 4, 4)].reshape(512, 128)

        @pl.loop(0, 2, unroll=2)
        def _(b):
            rows = pl.ds(pl.multiple_of(b * 512, 512), 512)
            for e2, l in enumerate((la, lb)):
                o = mm(l[rows], part, NT).astype(BF16)
                for e1 in range(4):
                    for i in range(16):
                        ot[
                            pl.ds(pl.multiple_of(q * 256 + (e2 * 4 + e1) * 32, 32), 32),
                            pl.ds(pl.multiple_of(b * 2048 + i * 128, 128), 128),
                        ] = o[i * 32 : i * 32 + 32, e1 * 128 : e1 * 128 + 128]

        @pl.when(q == 0)
        def _():
            for d in range(1, 4):
                n = (x + d) % 4
                copy_to(cr2.at[n], cr2.at[n], s2.at[0], r2.at[n], sibling).wait_recv()
            for d in (1, 2, 3, 0):
                zz = (z + d) % 4
                total = tr1[x, zz].astype(F32)
                for n in range(1, 4):
                    total = total + cr2[(x + n) % 4, zz].astype(F32)
                tr2[zz] = total.astype(BF16)
                if d:
                    z_right(d).start()

        @pl.when(q == 2)
        def _():
            for cp in lefts:
                cp.wait_recv()
            cl[c] = glx[c]
            total = cl[0].astype(F32)
            for n in range(1, 8):
                total = total + cl[n].astype(F32)
            tl[...] = total[:64].astype(BF16)
            bias[...] = total[64:]
            for d in range(1, 8):
                out_left(d).start()

        @pl.when(q == 1)
        def _():
            for d in range(1, 4):
                z_right(d).wait_recv()
            total = tr2[z].astype(F32)
            for n in range(1, 4):
                total = total + cr3[n].astype(F32)
            tr3[...] = total.astype(BF16)
            for cc in range(8):

                @unless((owner == r) & (c == cc))
                def _():
                    out_right(cc).start()

            @pl.when(owner == r)
            def _():
                fr[piece] = tr3[...]

        gw = mm(ot[pl.ds(pl.multiple_of(q * 256, 256), 256)], g_ref[...])
        for cc in range(2):
            for zz in range(4):
                at = cc * 128 + zz * 32
                sw[cc, q, zz] = gw[at : at + 32].astype(BF16)
        core_map(q).start()

        @pl.when(q > 0)
        def _():
            pass_map(q - 1)

    def z_map(d):
        zz = (z + d) % 4
        return copy_to(tw2.at[zz], cw3.at[d], s9.at[d], r9.at[d], (z_row(zz), c))

    def col_map(d):
        return copy_to(cw4.at[c], cw4.at[c], s10.at[d], r10.at[d], (r, (c + d) % 8))

    offset = off_ref[...]

    @pl.loop(0, 4)
    def _(b):
        update = mm(wpt_ref[...], ot[:, pl.ds(pl.multiple_of(b * 1024, 1024), 1024)])
        for i in range(8):
            at = pl.multiple_of(b * 1024 + i * 128, 128)
            pu_ref[pl.ds(at, 128)] = (update[:, i * 128 : i * 128 + 128].T + offset).astype(BF16)

        @pl.when(b == 0)
        def _():
            pass_map(3)

    put = pltpu.make_async_copy(pu_ref, pu_hbm, pu_sem)
    put.start()

    for d in range(1, 4):
        n = (x + d) % 4
        copy_to(cw2.at[n], cw2.at[n], s8.at[0], r8.at[n], sibling).wait_recv()
    for d in (1, 2, 3, 0):
        zz = (z + d) % 4
        total = tw1[x, zz].astype(F32)
        for n in range(1, 4):
            total = total + cw2[(x + n) % 4, zz].astype(F32)
        tw2[zz] = total.astype(BF16)
        if d:
            z_map(d).start()

    for d in range(1, 8):
        out_left(d).wait_recv()
    fl[c] = tl[...]
    for d in range(1, 4):
        z_map(d).wait_recv()
    total = tw2[z].astype(F32)
    for n in range(1, 4):
        total = total + cw3[n].astype(F32)
    cw4[c] = total.astype(BF16)
    for d in range(1, 8):
        col_map(d).start()
    for n in range(8):

        @unless((source(n) == r) & (goal == c))
        def _():
            copy_to(fr.at[n], fr.at[n], s4.at[n], r4.at[n], sibling).wait_recv()

    closing[...] = jnp.swapaxes(fr[...].reshape(16, 32, 128).astype(F32), 0, 1)

    def pair_grads(m):
        even, odd = closing[2 * m], closing[2 * m + 1]
        return jnp.concatenate(
            [
                fl[m // 2, pl.ds(pl.multiple_of((m % 2) * 32, 32), 32)],
                jnp.where(low16, even, pltpu.roll(odd, 64, 1)).astype(BF16),
                jnp.where(low16, pltpu.roll(even, 64, 1), odd).astype(BF16),
            ],
            axis=0,
        )

    acc[...] = jnp.zeros_like(acc)

    @pl.loop(0, 16, unroll=4)
    def _(m):
        grads = pair_grads(m)
        normed = (st[pl.ds(m * 2, 2)].reshape(128, 256) * gain).astype(BF16)
        acc[...] += mm(grads, normed)
        grads_all[m] = grads

    for n in range(2):
        for h in range(2):
            at = h * 32
            fs[n, at : at + 32] = acc[n * 32 : n * 32 + 32, h * 128 : h * 128 + 128]
        fs[n, 64:80] = bias[...]
    half = copy_to(fs.at[1 - core], fc1, s11.at[0], r11.at[0], sibling)
    half.start()

    def bring_adj(n):
        return pltpu.make_async_copy(
            adj_ref.at[n], adj_hbm.at[:, pl.ds(n * 8, 8)], adj_sem.at[n]
        )

    def adjoint(n):
        @pl.loop(0, 4, unroll=2)
        def _(p):
            m = n * 4 + p
            standard = st[pl.ds(m * 2, 2)].reshape(128, 256)
            inverse = inv[pl.ds(m * 2, 2)].reshape(128, 1)
            scaled = mm(grads_all[m], wt_ref[...], TN) * gain
            mean = jnp.mean(scaled, -1, keepdims=True)
            along = jnp.mean(scaled * standard, -1, keepdims=True)
            adj = inverse * (scaled - mean - standard * along)
            tall[pl.ds(p * 2, 2)] = adj.reshape(2, 64, 256)

        @pl.loop(0, 8, unroll=4)
        def _(b):
            rows = pl.ds(pl.multiple_of(b * 8, 8), 8)
            adj_ref[n, rows] = jnp.swapaxes(tall[:, rows], 0, 1)

        bring_adj(n).start()

    adjoint(0)
    half.wait_recv()
    fx[x] = (fs[core] + fc1[...]).astype(BF16)
    fxs = [
        copy_to(fx.at[x], fx.at[x], s13.at[d], r13.at[d], (x_row((x + d) % 4), c)) for d in range(1, 4)
    ]
    for cp in fxs:
        cp.start()
    adjoint(1)
    adjoint(2)
    for d in range(1, 8):
        col_map(d).wait_recv()
    total = cw4[0].astype(F32)
    for n in range(1, 8):
        total = total + cw4[n].astype(F32)
    wz[z] = total.astype(BF16)
    zs = [
        copy_to(wz.at[z], wz.at[z], s12.at[d], r12.at[d], (z_row((z + d) % 4), c)) for d in range(1, 4)
    ]
    for cp in zs:
        cp.start()
    for cp in fxs:
        cp.wait_recv()
    total = fx[0].astype(F32)
    for n in range(1, 4):
        total = total + fx[n].astype(F32)
    fz[z] = total.astype(BF16)
    fzs = [
        copy_to(fz.at[z], fz.at[z], s15.at[d], r15.at[d], (z_row((z + d) % 4), c)) for d in range(1, 4)
    ]
    for cp in fzs:
        cp.start()
    adjoint(3)
    for cp in zs:
        cp.wait_recv()
    wx[x] = wz[...]
    xs_ = [
        copy_to(wx.at[x], wx.at[x], s14.at[d], r14.at[d], (x_row((x + d) % 4), c)) for d in range(1, 4)
    ]
    for cp in xs_:
        cp.start()
    for cp in fzs:
        cp.wait_recv()
    total = fz[0].astype(F32)
    for n in range(1, 4):
        total = total + fz[n].astype(F32)
    ff[core] = total[:64]
    end = copy_to(ff.at[core], ff.at[core], s11.at[1], r11.at[1], sibling)
    end.start()
    bias_ref[...] = jnp.sum(total[64:], 0, keepdims=True)
    end.wait_recv()
    for n in range(2):
        for h in range(2):
            fac_ref[n, :, h * 128 : h * 128 + 128] = ff[n, h * 32 : h * 32 + 32]
    for cp in xs_:
        cp.wait_recv()
    last = copy_to(wx, wc, s16.at[0], r16.at[0], sibling)
    last.start()

    def spread(e2, parts):
        map_ref[:, pl.ds(pl.multiple_of(e2 * 16, 16), 16)] = jnp.swapaxes(
            parts.reshape(16, 32, 128).astype(F32), 0, 1
        )

    spread(core, wx[...])
    last.wait_recv()
    spread(1 - core, wc[...])

    for step in range(16):
        sends, cp = give(step)

        @pl.when(sends)
        def _():
            cp.wait_send()

    for q in range(4):
        core_right(q).wait_send()
        core_map(q).wait_send()

        @pl.when(x != q)
        def _():
            x_right(q).wait_send()
            x_map(q).wait_send()

        for m in range(2):
            swap(q, m).wait_send()
    for d in range(1, 4):
        z_right(d).wait_send()
        z_map(d).wait_send()
    for d in range(1, 8):
        out_left(d).wait_send()
        col_map(d).wait_send()
    for cc in range(8):

        @unless((owner == r) & (c == cc))
        def _():
            out_right(cc).wait_send()

    put.wait()
    for n in range(4):
        bring_adj(n).wait()
    for cp in lefts + zs + fxs + xs_ + fzs + [half, last, end]:
        cp.wait_send()


def run(x, gain, w1, w2, g, w, off):
    vm = pl.BlockSpec(memory_space=pltpu.VMEM)
    anywhere = pl.BlockSpec(memory_space=pl.ANY)

    def b16(*shape):
        return pltpu.VMEM(shape, BF16)

    def f32(*shape):
        return pltpu.VMEM(shape, F32)

    sems = []
    for n in (4, 4, 4, 8, 8, 8, 4, 4, 4, 8, 2, 4, 4, 4, 4, 1):
        sems += [pltpu.SemaphoreType.DMA((n,)), pltpu.SemaphoreType.DMA((n,))]
    return pl.pallas_call(
        kernel,
        out_shape=(
            jax.ShapeDtypeStruct((4096, 128), BF16),
            jax.ShapeDtypeStruct((64, 32, 256), F32),
            jax.ShapeDtypeStruct((2, 32, 256), F32),
            jax.ShapeDtypeStruct((1, 128), F32),
            jax.ShapeDtypeStruct((32, 32, 128), F32),
        ),
        in_specs=[vm, vm, vm, vm, anywhere, vm, vm],
        out_specs=(anywhere, anywhere, vm, vm, vm),
        scratch_shapes=[
            f32(32, 64, 256), f32(32, 64, 1), b16(4096, 128), b16(64, 256), b16(1024, 128), b16(128, 1024),
            b16(4096, 128), f32(32, 32, 128), f32(4, 64, 8, 256),
            b16(1024, 128), b16(1024, 128), b16(64, 1024), f32(1024, 128), f32(32, 16, 128),
            b16(16, 32, 128), b16(16, 4, 32, 128), b16(1024, 4096), b16(1024, 4096), b16(8, 80, 128),
            b16(2, 4, 4, 64, 128), b16(4, 4, 64, 128), b16(4, 4, 64, 128), b16(4, 4, 64, 128),
            b16(4, 64, 128), b16(4, 64, 128), b16(64, 128), b16(8, 64, 128),
            b16(2, 4, 4, 32, 128), b16(4, 4, 32, 128), b16(4, 4, 32, 128), b16(4, 4, 32, 128),
            b16(4, 32, 128), b16(4, 32, 128), b16(8, 32, 128), b16(4, 32, 128), b16(4, 4, 32, 128),
            b16(4, 4, 32, 128),
            b16(8, 80, 128), b16(64, 128), b16(8, 64, 128), f32(16, 128), f32(32, 16, 128), f32(64, 256),
            b16(16, 64, 128), f32(8, 64, 256), f32(2, 80, 128), f32(80, 128), b16(4, 80, 128), b16(4, 80, 128), f32(2, 64, 128),
            pltpu.SemaphoreType.DMA((16,)), pltpu.SemaphoreType.DMA((8,)),
            pltpu.SemaphoreType.DMA((8,)), pltpu.SemaphoreType.DMA((8,)), pltpu.SemaphoreType.DMA,
            pltpu.SemaphoreType.DMA, pltpu.SemaphoreType.DMA, pltpu.SemaphoreType.DMA((4,)),
            *sems,
        ],
        compiler_params=pltpu.CompilerParams(
            collective_id=0, has_side_effects=True, vmem_limit_bytes=56 << 20
        ),
        name="outer_product_mean",
    )(x, gain, w1, w2, g, w, off)


def per_device(
    sequence_stack,
    feature_multiplier,
    first_factor_map,
    second_factor_map,
    emitted_map,
    emitted_offset,
    upstream_adjoint,
):
    pu, adj, fac, bias, w = run(
        sequence_stack,
        feature_multiplier.reshape(1, 256),
        first_factor_map.T,
        second_factor_map.T,
        upstream_adjoint.reshape(4096, 128),
        emitted_map,
        emitted_offset.reshape(1, 128),
    )
    return (
        pu.reshape(32, 128, 128),
        adj,
        fac.transpose(0, 2, 1),
        w.reshape(1024, 128),
        bias.reshape(128),
    )


def solution(mesh):
    return jax.shard_map(
        per_device,
        mesh=mesh,
        in_specs=(P(None, "row", None), P(), P(), P(), P(), P(), P("row", "col", None)),
        out_specs=(P("row", "col", None), P(None, "row", None), P(), P(), P()),
        check_vma=False,
    )
```

```python
import jax
import jax.numpy as jnp
from jax import lax
from jax.experimental import pallas as pl
from jax.experimental.pallas import tpu as pltpu
from jax.sharding import PartitionSpec as P

MESH = pl.DeviceIdType.MESH
F32 = jnp.float32
BF16 = jnp.bfloat16
NN = (((1,), (0,)), ((), ()))
NT = (((1,), (1,)), ((), ()))
TN = (((0,), (0,)), ((), ()))


def mm(a, b, dims=NN):
    return lax.dot_general(a, b, dims, preferred_element_type=F32)


def low_lanes(shape):
    return lax.broadcasted_iota(jnp.int32, shape, 1) < 64


def normalise(x):
    average = jnp.mean(x, -1, keepdims=True)
    centered = x - average
    variance = jnp.mean(centered * centered, -1, keepdims=True)
    inverse = lax.rsqrt(variance + 1e-05)
    return centered * inverse, inverse


def place():
    r = lax.axis_index("row")
    return r, lax.axis_index("col"), r // 8, (r // 2) % 4, r % 2


def serving_half(z, x, z0, zh):
    gap = jnp.abs(z - z0)
    other = jnp.where(gap == 3, 1, jnp.where(gap == 2, (z + x) % 2, 0))
    return (zh + other) % 2


def copy_to(src, dst, send_sem, recv_sem, device):
    return pltpu.make_async_remote_copy(
        src_ref=src,
        dst_ref=dst,
        send_sem=send_sem,
        recv_sem=recv_sem,
        device_id=device,
        device_id_type=MESH,
    )


def unless(condition):
    return pl.when(jnp.logical_not(condition))


def kernel(
    x_ref, gain_ref, w1_ref, w2_ref, g_hbm, w_ref, off_ref,
    pu_hbm, adj_hbm, fac_ref, bias_ref, map_ref,
    st, inv, g_ref, wt_ref, wp_ref, wpt_ref, pu_ref, turn, adj_ref,
    la, lb, lt, left, right, rb, land, dt, ot, glx,
    sr, cr1, tr1, cr2, tr2, cr3, tr3, fr,
    sw, cw1, tw1, cw2, tw2, cw3, cw4, wz, wx, wc,
    cl, tl, fl, bias, closing, acc, grads_all, tall, fs, fc1, fx, fz, ff,
    gs, gd, ks, kd, own_sem, g_sem, pu_sem, adj_sem,
    s1, r1, s2, r2, s3, r3, s4, r4, s5, r5, s6, r6, s7, r7, s8, r8, s9, r9,
    s10, r10, s11, r11, s12, r12, s13, r13, s14, r14, s15, r15, s16, r16,
):
    r, c, z, x, core = place()
    zh, y = c // 4, c % 4
    sibling = (r + 1 - 2 * core, c)
    goal = r // 4
    k = core + 2 * (z // 2)
    owner = 4 * c + k
    piece = x * 2 + z % 2

    def x_row(xx):
        return z * 8 + xx * 2 + core

    def z_row(zz):
        return zz * 8 + x * 2 + core

    def giver(m, q):
        row = 4 * c + core + 2 * m
        return row, serving_half(z, x, row // 8, zh) * 4 + q

    def source(n):
        return (((r % 4) // 2) * 2 + n % 2) * 8 + (n // 2) * 2 + r % 2

    def chip(step):
        dz, dx = (z + step // 4) % 4, (x + step % 4) % 4
        serves = serving_half(dz, dx, z, goal // 4) == zh
        return dz, dx, serves, (goal == c) & (step == 0)

    barrier = pltpu.get_barrier_semaphore()

    def signal(device):
        pl.semaphore_signal(barrier, inc=1, device_id=device, device_id_type=MESH)

    signal(sibling)
    for d in range(1, 4):
        signal((x_row((x + d) % 4), c))
        signal((z_row((z + d) % 4), c))
    for d in range(1, 8):
        signal((r, (c + d) % 8))
    for n in range(8):

        @unless((source(n) == r) & (goal == c))
        def _():
            signal((source(n), goal))

        row, col = giver(n % 2, n // 2)

        @unless((row == r) & (col == c))
        def _():
            signal((row, col))

    bring = pltpu.make_async_copy(g_hbm, g_ref, g_sem)
    bring.start()

    gain = gain_ref[...]
    wt = jnp.concatenate([w1_ref[...], w2_ref[...]], axis=0)
    wt_ref[...] = wt

    @pl.loop(0, 8, unroll=4)
    def _(b):
        rows = pl.ds(pl.multiple_of(b * 8, 8), 8)
        for h in range(2):
            xs = x_ref[rows, h * 16 : h * 16 + 16].astype(F32)
            st[h * 16 : h * 16 + 16, rows] = jnp.swapaxes(xs, 0, 1)

    low32 = low_lanes((32, 128))
    low16 = low_lanes((16, 128))

    @pl.loop(0, 8, unroll=2)
    def _(b):
        standard, inverse = normalise(st[pl.ds(b * 4, 4)].reshape(256, 256))
        st[pl.ds(b * 4, 4)] = standard.reshape(4, 64, 256)
        inv[pl.ds(b * 4, 4)] = inverse.reshape(4, 64, 1)
        normed = (standard * gain).astype(BF16)
        both = mm(wt, normed, NT).astype(BF16).astype(F32)
        for p in range(2):
            tile = both[:, p * 128 : (p + 1) * 128]
            turned = pltpu.roll(tile, 64, 1)
            row = pl.multiple_of(b * 128 + p * 64, 64)
            scaled, scaled_turned = tile[:32] * (1 / 64), turned[:32] * (1 / 64)
            zero = jnp.zeros_like(scaled)
            la[pl.ds(row, 32)] = jnp.where(low32, scaled, zero).astype(BF16)
            lb[pl.ds(row, 32)] = jnp.where(low32, zero, scaled_turned).astype(BF16)
            la[pl.ds(row + 32, 32)] = jnp.where(low32, scaled_turned, zero).astype(BF16)
            lb[pl.ds(row + 32, 32)] = jnp.where(low32, zero, scaled).astype(BF16)
            left[pl.ds(row, 32)] = scaled
            left[pl.ds(row + 32, 32)] = scaled_turned
            j = b * 4 + p * 2
            right[j] = jnp.where(low16, tile[32:48], turned[48:64])
            right[j + 1] = jnp.where(low16, turned[32:48], tile[48:64])

    rb[...] = jnp.swapaxes(right[...], 0, 1).astype(BF16)

    count = jnp.int32(14 + 8) - jnp.where(owner == r, 1, 0)
    for step in range(16):
        dz, dx, serves, myself = chip(step)
        count = count + jnp.where(serves & jnp.logical_not(myself), 1, 0)
    pl.semaphore_wait(barrier, count)

    mine = rb.at[pl.ds(y * 4, 4)]
    slot = land.at[pl.ds(y * 4, 4), r % 4]

    def give(step):
        dz, dx, serves, myself = chip(step)
        cp = copy_to(
            mine, slot, gs.at[step], gd.at[((r % 4) // 2) * 4 + y], (dz * 8 + dx * 2 + core, goal)
        )
        return serves & jnp.logical_not(myself), cp

    for step in range(16):
        sends, cp = give(step)

        @pl.when(sends)
        def _():
            cp.start()

    @pl.when((goal == c) & (chip(0)[2]))
    def _():
        own = pltpu.make_async_copy(mine, slot, own_sem)
        own.start()
        own.wait()

    turn[...] = jnp.swapaxes(w_ref[...].reshape(32, 32, 128).astype(F32), 0, 1)
    for q in range(4):
        for e2 in range(2):
            at = q * 256 + e2 * 128
            tile = turn[e2 * 16 + q * 4 : e2 * 16 + q * 4 + 4].reshape(128, 128)
            wp_ref[at : at + 128] = tile.astype(BF16)
            wpt_ref[:, at : at + 128] = tile.T.astype(BF16)
    for b in range(8):
        lt[:, b * 128 : (b + 1) * 128] = left[b * 128 : (b + 1) * 128].T[:64].astype(BF16)

    bring.wait()

    def core_right(q):
        return copy_to(sr.at[1 - core, q], cr1.at[q], s1.at[q], r1.at[q], sibling)

    def x_right(q):
        return copy_to(tr1.at[q], cr2.at[x], s2.at[q], r2.at[x], (x_row(q), c))

    def pass_right(q):
        core_right(q).wait_recv()
        tr1[q] = (sr[core, q].astype(F32) + cr1[q].astype(F32)).astype(BF16)

        @pl.when(x != q)
        def _():
            x_right(q).start()

    @pl.loop(0, 4)
    def _(q):
        wq = wp_ref[pl.ds(pl.multiple_of(q * 256, 256), 256)]

        @pl.loop(0, 2, unroll=2)
        def _(b):
            g = g_ref[pl.ds(pl.multiple_of(b * 2048, 2048), 2048)]
            d = mm(wq, g, NT).astype(BF16)
            for e in range(8):
                for i in range(16):
                    dt[
                        pl.ds(pl.multiple_of(b * 512 + i * 32, 32), 32),
                        pl.ds(pl.multiple_of(q * 1024 + e * 128, 128), 128),
                    ] = d[e * 32 : e * 32 + 32, i * 128 : i * 128 + 128]

        gr = mm(lt[...], dt[:, pl.ds(pl.multiple_of(q * 1024, 1024), 1024)])
        for e1 in range(4):
            tile = jnp.concatenate(
                [gr[:, e1 * 128 : e1 * 128 + 128], gr[:, 512 + e1 * 128 : 640 + e1 * 128]], axis=0
            )
            turned = tile.T.astype(BF16)
            for kk in range(4):
                at = (e1 % 2) * 32
                sr[kk % 2, q, (kk // 2) * 2 + e1 // 2, at : at + 32] = turned[kk * 32 : kk * 32 + 32]
        core_right(q).start()

        @pl.when(q > 0)
        def _():
            pass_right(q - 1)

    def swap(q, m):
        there = land.at[pl.ds(q * 4, 4), core + 2 * m]
        return copy_to(there, there, ks.at[m * 4 + q], kd.at[m * 4 + q], sibling)

    for q in range(4):
        for m in range(2):
            row, col = giver(m, q)
            there = land.at[pl.ds(q * 4, 4), core + 2 * m]

            @unless((row == r) & (col == c))
            def _():
                copy_to(there, there, ks.at[m * 4 + q], gd.at[m * 4 + q], sibling).wait_recv()

            swap(q, m).start()
    pass_right(3)
    for q in range(4):
        for m in range(2):
            there = land.at[pl.ds(q * 4, 4), 1 - core + 2 * m]
            copy_to(there, there, ks.at[m * 4 + q], kd.at[m * 4 + q], sibling).wait_recv()

    bias[...] = jnp.zeros_like(bias)

    @pl.loop(0, 4, unroll=2)
    def _(b):
        rows = pl.ds(pl.multiple_of(b * 256, 256), 256)
        first = jnp.zeros((256, 128), F32)
        second = jnp.zeros((256, 128), F32)
        for q in range(4):
            part = land[q * 4 : q * 4 + 4].reshape(512, 128)
            first = first + mm(dt[rows, q * 1024 : q * 1024 + 512], part)
            second = second + mm(dt[rows, q * 1024 + 512 : q * 1024 + 1024], part)
        for m in range(4):
            even, odd = slice(m * 64, m * 64 + 32), slice(m * 64 + 32, m * 64 + 64)
            one = first[even] + pltpu.roll(second[even], 64, 1)
            two = second[odd] + pltpu.roll(first[odd], 64, 1)
            at = (m % 2) * 32
            glx[b * 2 + m // 2, at : at + 32] = (jnp.where(low32, one, two) * (1 / 64)).astype(BF16)
        g = g_ref[pl.ds(pl.multiple_of(b * 1024, 1024), 1024)]
        bias[...] += jnp.sum(g.astype(F32).reshape(64, 16, 128), 0)

    for n in range(8):
        glx[n, 64:80] = bias[...].astype(BF16)
    lefts = []
    for d in range(1, 8):
        cc = (c + d) % 8
        lefts.append(copy_to(glx.at[cc], cl.at[c], s5.at[d], r5.at[d], (r, cc)))
        lefts[-1].start()

    def core_map(q):
        return copy_to(sw.at[1 - core, q], cw1.at[q], s7.at[q], r7.at[q], sibling)

    def x_map(q):
        return copy_to(tw1.at[q], cw2.at[x], s8.at[q], r8.at[x], (x_row(q), c))

    def pass_map(q):
        core_map(q).wait_recv()
        tw1[q] = (sw[core, q].astype(F32) + cw1[q].astype(F32)).astype(BF16)

        @pl.when(x != q)
        def _():
            x_map(q).start()

    def z_right(d):
        zz = (z + d) % 4
        return copy_to(tr2.at[zz], cr3.at[d], s3.at[d], r3.at[d], (z_row(zz), c))

    def out_right(cc):
        return copy_to(tr3, fr.at[piece], s4.at[cc], r4.at[piece], (owner, cc))

    def out_left(d):
        return copy_to(tl, fl.at[c], s6.at[d], r6.at[d], (r, (c + d) % 8))

    @pl.loop(0, 4)
    def _(q):
        part = land[pl.ds(q * 4, 4)].reshape(512, 128)

        @pl.loop(0, 2, unroll=2)
        def _(b):
            rows = pl.ds(pl.multiple_of(b * 512, 512), 512)
            for e2, l in enumerate((la, lb)):
                o = mm(l[rows], part, NT).astype(BF16)
                for e1 in range(4):
                    for i in range(16):
                        ot[
                            pl.ds(pl.multiple_of(q * 256 + (e2 * 4 + e1) * 32, 32), 32),
                            pl.ds(pl.multiple_of(b * 2048 + i * 128, 128), 128),
                        ] = o[i * 32 : i * 32 + 32, e1 * 128 : e1 * 128 + 128]

        @pl.when(q == 1)
        def _():
            for d in range(1, 4):
                n = (x + d) % 4
                copy_to(cr2.at[n], cr2.at[n], s2.at[0], r2.at[n], sibling).wait_recv()
            for d in (1, 2, 3, 0):
                zz = (z + d) % 4
                total = tr1[x, zz].astype(F32)
                for n in range(1, 4):
                    total = total + cr2[(x + n) % 4, zz].astype(F32)
                tr2[zz] = total.astype(BF16)
                if d:
                    z_right(d).start()

        @pl.when(q == 3)
        def _():
            for cp in lefts:
                cp.wait_recv()
            cl[c] = glx[c]
            total = cl[0].astype(F32)
            for n in range(1, 8):
                total = total + cl[n].astype(F32)
            tl[...] = total[:64].astype(BF16)
            bias[...] = total[64:]
            for d in range(1, 8):
                out_left(d).start()

        @pl.when(q == 2)
        def _():
            for d in range(1, 4):
                z_right(d).wait_recv()
            total = tr2[z].astype(F32)
            for n in range(1, 4):
                total = total + cr3[n].astype(F32)
            tr3[...] = total.astype(BF16)
            for cc in range(8):

                @unless((owner == r) & (c == cc))
                def _():
                    out_right(cc).start()

            @pl.when(owner == r)
            def _():
                fr[piece] = tr3[...]

        gw = mm(ot[pl.ds(pl.multiple_of(q * 256, 256), 256)], g_ref[...])
        for cc in range(2):
            for zz in range(4):
                at = cc * 128 + zz * 32
                sw[cc, q, zz] = gw[at : at + 32].astype(BF16)
        core_map(q).start()

        @pl.when(q > 0)
        def _():
            pass_map(q - 1)

    def z_map(d):
        zz = (z + d) % 4
        return copy_to(tw2.at[zz], cw3.at[d], s9.at[d], r9.at[d], (z_row(zz), c))

    def col_map(d):
        return copy_to(cw4.at[c], cw4.at[c], s10.at[d], r10.at[d], (r, (c + d) % 8))

    offset = off_ref[...]

    @pl.loop(0, 4)
    def _(b):
        update = mm(wpt_ref[...], ot[:, pl.ds(pl.multiple_of(b * 1024, 1024), 1024)])
        for i in range(8):
            at = pl.multiple_of(b * 1024 + i * 128, 128)
            pu_ref[pl.ds(at, 128)] = (update[:, i * 128 : i * 128 + 128].T + offset).astype(BF16)

        @pl.when(b == 0)
        def _():
            pass_map(3)

    put = pltpu.make_async_copy(pu_ref, pu_hbm, pu_sem)
    put.start()

    for d in range(1, 4):
        n = (x + d) % 4
        copy_to(cw2.at[n], cw2.at[n], s8.at[0], r8.at[n], sibling).wait_recv()
    for d in (1, 2, 3, 0):
        zz = (z + d) % 4
        total = tw1[x, zz].astype(F32)
        for n in range(1, 4):
            total = total + cw2[(x + n) % 4, zz].astype(F32)
        tw2[zz] = total.astype(BF16)
        if d:
            z_map(d).start()

    for d in range(1, 8):
        out_left(d).wait_recv()
    fl[c] = tl[...]
    for d in range(1, 4):
        z_map(d).wait_recv()
    total = tw2[z].astype(F32)
    for n in range(1, 4):
        total = total + cw3[n].astype(F32)
    cw4[c] = total.astype(BF16)
    for d in range(1, 8):
        col_map(d).start()
    for n in range(8):

        @unless((source(n) == r) & (goal == c))
        def _():
            copy_to(fr.at[n], fr.at[n], s4.at[n], r4.at[n], sibling).wait_recv()

    closing[...] = jnp.swapaxes(fr[...].reshape(16, 32, 128).astype(F32), 0, 1)

    def pair_grads(m):
        even, odd = closing[2 * m], closing[2 * m + 1]
        return jnp.concatenate(
            [
                fl[m // 2, pl.ds(pl.multiple_of((m % 2) * 32, 32), 32)],
                jnp.where(low16, even, pltpu.roll(odd, 64, 1)).astype(BF16),
                jnp.where(low16, pltpu.roll(even, 64, 1), odd).astype(BF16),
            ],
            axis=0,
        )

    acc[...] = jnp.zeros_like(acc)

    @pl.loop(0, 16, unroll=4)
    def _(m):
        grads = pair_grads(m)
        normed = (st[pl.ds(m * 2, 2)].reshape(128, 256) * gain).astype(BF16)
        acc[...] += mm(grads, normed)
        grads_all[m] = grads

    for n in range(2):
        for h in range(2):
            at = h * 32
            fs[n, at : at + 32] = acc[n * 32 : n * 32 + 32, h * 128 : h * 128 + 128]
        fs[n, 64:80] = bias[...]
    half = copy_to(fs.at[1 - core], fc1, s11.at[0], r11.at[0], sibling)
    half.start()

    def bring_adj(n):
        return pltpu.make_async_copy(
            adj_ref.at[n], adj_hbm.at[:, pl.ds(n * 8, 8)], adj_sem.at[n]
        )

    def adjoint(n):
        @pl.loop(0, 4, unroll=2)
        def _(p):
            m = n * 4 + p
            standard = st[pl.ds(m * 2, 2)].reshape(128, 256)
            inverse = inv[pl.ds(m * 2, 2)].reshape(128, 1)
            scaled = mm(grads_all[m], wt_ref[...], TN) * gain
            mean = jnp.mean(scaled, -1, keepdims=True)
            along = jnp.mean(scaled * standard, -1, keepdims=True)
            adj = inverse * (scaled - mean - standard * along)
            tall[pl.ds(p * 2, 2)] = adj.reshape(2, 64, 256)

        @pl.loop(0, 8, unroll=4)
        def _(b):
            rows = pl.ds(pl.multiple_of(b * 8, 8), 8)
            adj_ref[n, rows] = jnp.swapaxes(tall[:, rows], 0, 1)

        bring_adj(n).start()

    adjoint(0)
    half.wait_recv()
    fx[x] = (fs[core] + fc1[...]).astype(BF16)
    fxs = [
        copy_to(fx.at[x], fx.at[x], s13.at[d], r13.at[d], (x_row((x + d) % 4), c)) for d in range(1, 4)
    ]
    for cp in fxs:
        cp.start()
    adjoint(1)
    adjoint(2)
    for d in range(1, 8):
        col_map(d).wait_recv()
    total = cw4[0].astype(F32)
    for n in range(1, 8):
        total = total + cw4[n].astype(F32)
    wz[z] = total.astype(BF16)
    zs = [
        copy_to(wz.at[z], wz.at[z], s12.at[d], r12.at[d], (z_row((z + d) % 4), c)) for d in range(1, 4)
    ]
    for cp in zs:
        cp.start()
    for cp in fxs:
        cp.wait_recv()
    total = fx[0].astype(F32)
    for n in range(1, 4):
        total = total + fx[n].astype(F32)
    fz[z] = total.astype(BF16)
    fzs = [
        copy_to(fz.at[z], fz.at[z], s15.at[d], r15.at[d], (z_row((z + d) % 4), c)) for d in range(1, 4)
    ]
    for cp in fzs:
        cp.start()
    adjoint(3)
    for cp in zs:
        cp.wait_recv()
    wx[x] = wz[...]
    xs_ = [
        copy_to(wx.at[x], wx.at[x], s14.at[d], r14.at[d], (x_row((x + d) % 4), c)) for d in range(1, 4)
    ]
    for cp in xs_:
        cp.start()
    for cp in fzs:
        cp.wait_recv()
    total = fz[0].astype(F32)
    for n in range(1, 4):
        total = total + fz[n].astype(F32)
    ff[core] = total[:64]
    end = copy_to(ff.at[core], ff.at[core], s11.at[1], r11.at[1], sibling)
    end.start()
    bias_ref[...] = jnp.sum(total[64:], 0, keepdims=True)
    end.wait_recv()
    for n in range(2):
        for h in range(2):
            fac_ref[n, :, h * 128 : h * 128 + 128] = ff[n, h * 32 : h * 32 + 32]
    for cp in xs_:
        cp.wait_recv()
    last = copy_to(wx, wc, s16.at[0], r16.at[0], sibling)
    last.start()

    def spread(e2, parts):
        map_ref[:, pl.ds(pl.multiple_of(e2 * 16, 16), 16)] = jnp.swapaxes(
            parts.reshape(16, 32, 128).astype(F32), 0, 1
        )

    spread(core, wx[...])
    last.wait_recv()
    spread(1 - core, wc[...])

    for step in range(16):
        sends, cp = give(step)

        @pl.when(sends)
        def _():
            cp.wait_send()

    for q in range(4):
        core_right(q).wait_send()
        core_map(q).wait_send()

        @pl.when(x != q)
        def _():
            x_right(q).wait_send()
            x_map(q).wait_send()

        for m in range(2):
            swap(q, m).wait_send()
    for d in range(1, 4):
        z_right(d).wait_send()
        z_map(d).wait_send()
    for d in range(1, 8):
        out_left(d).wait_send()
        col_map(d).wait_send()
    for cc in range(8):

        @unless((owner == r) & (c == cc))
        def _():
            out_right(cc).wait_send()

    put.wait()
    for n in range(4):
        bring_adj(n).wait()
    for cp in lefts + zs + fxs + xs_ + fzs + [half, last, end]:
        cp.wait_send()


def run(x, gain, w1, w2, g, w, off):
    vm = pl.BlockSpec(memory_space=pltpu.VMEM)
    anywhere = pl.BlockSpec(memory_space=pl.ANY)

    def b16(*shape):
        return pltpu.VMEM(shape, BF16)

    def f32(*shape):
        return pltpu.VMEM(shape, F32)

    sems = []
    for n in (4, 4, 4, 8, 8, 8, 4, 4, 4, 8, 2, 4, 4, 4, 4, 1):
        sems += [pltpu.SemaphoreType.DMA((n,)), pltpu.SemaphoreType.DMA((n,))]
    return pl.pallas_call(
        kernel,
        out_shape=(
            jax.ShapeDtypeStruct((4096, 128), BF16),
            jax.ShapeDtypeStruct((64, 32, 256), F32),
            jax.ShapeDtypeStruct((2, 32, 256), F32),
            jax.ShapeDtypeStruct((1, 128), F32),
            jax.ShapeDtypeStruct((32, 32, 128), F32),
        ),
        in_specs=[vm, vm, vm, vm, anywhere, vm, vm],
        out_specs=(anywhere, anywhere, vm, vm, vm),
        scratch_shapes=[
            f32(32, 64, 256), f32(32, 64, 1), b16(4096, 128), b16(64, 256), b16(1024, 128), b16(128, 1024),
            b16(4096, 128), f32(32, 32, 128), f32(4, 64, 8, 256),
            b16(1024, 128), b16(1024, 128), b16(64, 1024), f32(1024, 128), f32(32, 16, 128),
            b16(16, 32, 128), b16(16, 4, 32, 128), b16(1024, 4096), b16(1024, 4096), b16(8, 80, 128),
            b16(2, 4, 4, 64, 128), b16(4, 4, 64, 128), b16(4, 4, 64, 128), b16(4, 4, 64, 128),
            b16(4, 64, 128), b16(4, 64, 128), b16(64, 128), b16(8, 64, 128),
            b16(2, 4, 4, 32, 128), b16(4, 4, 32, 128), b16(4, 4, 32, 128), b16(4, 4, 32, 128),
            b16(4, 32, 128), b16(4, 32, 128), b16(8, 32, 128), b16(4, 32, 128), b16(4, 4, 32, 128),
            b16(4, 4, 32, 128),
            b16(8, 80, 128), b16(64, 128), b16(8, 64, 128), f32(16, 128), f32(32, 16, 128), f32(64, 256),
            b16(16, 64, 128), f32(8, 64, 256), f32(2, 80, 128), f32(80, 128), b16(4, 80, 128), b16(4, 80, 128), f32(2, 64, 128),
            pltpu.SemaphoreType.DMA((16,)), pltpu.SemaphoreType.DMA((8,)),
            pltpu.SemaphoreType.DMA((8,)), pltpu.SemaphoreType.DMA((8,)), pltpu.SemaphoreType.DMA,
            pltpu.SemaphoreType.DMA, pltpu.SemaphoreType.DMA, pltpu.SemaphoreType.DMA((4,)),
            *sems,
        ],
        compiler_params=pltpu.CompilerParams(
            collective_id=0, has_side_effects=True, vmem_limit_bytes=56 << 20
        ),
        name="outer_product_mean",
    )(x, gain, w1, w2, g, w, off)


def hand_over_kernel(*refs):
    sources, goals, sem = refs[:5], refs[5:10], refs[10]
    copies = []
    for source, goal, parts in zip(sources, goals, (4, 8, 1, 1, 1)):
        rows = source.shape[0] // parts
        for n in range(parts):
            at = pl.ds(n * rows, rows)
            copies.append((source.at[at], goal.at[at]))
    copies = [pltpu.make_async_copy(a, b, sem.at[n]) for n, (a, b) in enumerate(copies)]
    for cp in copies:
        cp.start()
    for cp in copies:
        cp.wait()


def hand_over(*arrays):
    anywhere = pl.BlockSpec(memory_space=pl.ANY)
    return pl.pallas_call(
        hand_over_kernel,
        out_shape=tuple(jax.ShapeDtypeStruct(a.shape, a.dtype) for a in arrays),
        in_specs=[anywhere] * 5,
        out_specs=(anywhere,) * 5,
        scratch_shapes=[pltpu.SemaphoreType.DMA((15,))],
        compiler_params=pltpu.CompilerParams(vmem_limit_bytes=62 << 20),
        name="hand_over",
    )(*arrays)


def per_device(
    sequence_stack,
    feature_multiplier,
    first_factor_map,
    second_factor_map,
    emitted_map,
    emitted_offset,
    upstream_adjoint,
):
    pu, adj, fac, bias, w = run(
        sequence_stack,
        feature_multiplier.reshape(1, 256),
        first_factor_map.T,
        second_factor_map.T,
        upstream_adjoint.reshape(4096, 128),
        emitted_map,
        emitted_offset.reshape(1, 128),
    )
    pu, adj, fac, bias, w = hand_over(pu, adj, fac, bias, w)
    return (
        pu.reshape(32, 128, 128),
        adj,
        fac.transpose(0, 2, 1),
        w.reshape(1024, 128),
        bias.reshape(128),
    )


def solution(mesh):
    return jax.shard_map(
        per_device,
        mesh=mesh,
        in_specs=(P(None, "row", None), P(), P(), P(), P(), P(), P("row", "col", None)),
        out_specs=(P("row", "col", None), P(None, "row", None), P(), P(), P()),
        check_vma=False,
    )
```

```python
import jax
import jax.numpy as jnp
from jax import lax
from jax.experimental import pallas as pl
from jax.experimental.pallas import tpu as pltpu
from jax.sharding import PartitionSpec as P

MESH = pl.DeviceIdType.MESH
F32 = jnp.float32
BF16 = jnp.bfloat16
NN = (((1,), (0,)), ((), ()))
NT = (((1,), (1,)), ((), ()))
TN = (((0,), (0,)), ((), ()))


def mm(a, b, dims=NN):
    return lax.dot_general(a, b, dims, preferred_element_type=F32)


def low_lanes(shape):
    return lax.broadcasted_iota(jnp.int32, shape, 1) < 64


def normalise(x):
    average = jnp.mean(x, -1, keepdims=True)
    centered = x - average
    variance = jnp.mean(centered * centered, -1, keepdims=True)
    inverse = lax.rsqrt(variance + 1e-05)
    return centered * inverse, inverse


def place():
    r = lax.axis_index("row")
    return r, lax.axis_index("col"), r // 8, (r // 2) % 4, r % 2


def serving_half(z, x, z0, zh):
    gap = jnp.abs(z - z0)
    other = jnp.where(gap == 3, 1, jnp.where(gap == 2, (z + x) % 2, 0))
    return (zh + other) % 2


def copy_to(src, dst, send_sem, recv_sem, device):
    return pltpu.make_async_remote_copy(
        src_ref=src,
        dst_ref=dst,
        send_sem=send_sem,
        recv_sem=recv_sem,
        device_id=device,
        device_id_type=MESH,
    )


def unless(condition):
    return pl.when(jnp.logical_not(condition))


def kernel(
    x_ref, gain_ref, w1_ref, w2_ref, g_hbm, w_ref, off_ref,
    pu_hbm, adj_hbm, fac_ref, bias_ref, map_ref,
    st, inv, g_ref, wt_ref, wp_ref, wpt_ref, pu_ref, turn, adj_ref,
    la, lb, lt, left, right, rb, land, dt, ot, glx,
    sr, cr1, tr1, cr2, tr2, cr3, tr3, fr,
    sw, cw1, tw1, cw2, tw2, cw3, cw4, wz, wx, wc,
    cl, tl, fl, bias, closing, acc, grads_all, tall, fs, fc1, fx, fz, ff,
    gs, gd, ks, kd, own_sem, g_sem, pu_sem, adj_sem,
    s1, r1, s2, r2, s3, r3, s4, r4, s5, r5, s6, r6, s7, r7, s8, r8, s9, r9,
    s10, r10, s11, r11, s12, r12, s13, r13, s14, r14, s15, r15, s16, r16,
):
    r, c, z, x, core = place()
    zh, y = c // 4, c % 4
    sibling = (r + 1 - 2 * core, c)
    goal = r // 4
    k = core + 2 * (z // 2)
    owner = 4 * c + k
    piece = x * 2 + z % 2

    def x_row(xx):
        return z * 8 + xx * 2 + core

    def z_row(zz):
        return zz * 8 + x * 2 + core

    def giver(m, q):
        row = 4 * c + core + 2 * m
        return row, serving_half(z, x, row // 8, zh) * 4 + q

    def source(n):
        return (((r % 4) // 2) * 2 + n % 2) * 8 + (n // 2) * 2 + r % 2

    def chip(step):
        dz, dx = (z + step // 4) % 4, (x + step % 4) % 4
        serves = serving_half(dz, dx, z, goal // 4) == zh
        return dz, dx, serves, (goal == c) & (step == 0)

    barrier = pltpu.get_barrier_semaphore()

    def signal(device):
        pl.semaphore_signal(barrier, inc=1, device_id=device, device_id_type=MESH)

    signal(sibling)
    for d in range(1, 4):
        signal((x_row((x + d) % 4), c))
        signal((z_row((z + d) % 4), c))
    for d in range(1, 8):
        signal((r, (c + d) % 8))
    for n in range(8):

        @unless((source(n) == r) & (goal == c))
        def _():
            signal((source(n), goal))

        row, col = giver(n % 2, n // 2)

        @unless((row == r) & (col == c))
        def _():
            signal((row, col))

    bring = pltpu.make_async_copy(g_hbm, g_ref, g_sem)
    bring.start()

    gain = gain_ref[...]
    wt = jnp.concatenate([w1_ref[...], w2_ref[...]], axis=0)
    wt_ref[...] = wt

    @pl.loop(0, 8, unroll=4)
    def _(b):
        rows = pl.ds(pl.multiple_of(b * 8, 8), 8)
        for h in range(2):
            xs = x_ref[rows, h * 16 : h * 16 + 16].astype(F32)
            st[h * 16 : h * 16 + 16, rows] = jnp.swapaxes(xs, 0, 1)

    low32 = low_lanes((32, 128))
    low16 = low_lanes((16, 128))

    @pl.loop(0, 8, unroll=2)
    def _(b):
        standard, inverse = normalise(st[pl.ds(b * 4, 4)].reshape(256, 256))
        st[pl.ds(b * 4, 4)] = standard.reshape(4, 64, 256)
        inv[pl.ds(b * 4, 4)] = inverse.reshape(4, 64, 1)
        normed = (standard * gain).astype(BF16)
        both = mm(wt, normed, NT).astype(BF16).astype(F32)
        for p in range(2):
            tile = both[:, p * 128 : (p + 1) * 128]
            turned = pltpu.roll(tile, 64, 1)
            row = pl.multiple_of(b * 128 + p * 64, 64)
            scaled, scaled_turned = tile[:32] * (1 / 64), turned[:32] * (1 / 64)
            zero = jnp.zeros_like(scaled)
            la[pl.ds(row, 32)] = jnp.where(low32, scaled, zero).astype(BF16)
            lb[pl.ds(row, 32)] = jnp.where(low32, zero, scaled_turned).astype(BF16)
            la[pl.ds(row + 32, 32)] = jnp.where(low32, scaled_turned, zero).astype(BF16)
            lb[pl.ds(row + 32, 32)] = jnp.where(low32, zero, scaled).astype(BF16)
            left[pl.ds(row, 32)] = scaled
            left[pl.ds(row + 32, 32)] = scaled_turned
            j = b * 4 + p * 2
            right[j] = jnp.where(low16, tile[32:48], turned[48:64])
            right[j + 1] = jnp.where(low16, turned[32:48], tile[48:64])

    rb[...] = jnp.swapaxes(right[...], 0, 1).astype(BF16)

    count = jnp.int32(14 + 8) - jnp.where(owner == r, 1, 0)
    for step in range(16):
        dz, dx, serves, myself = chip(step)
        count = count + jnp.where(serves & jnp.logical_not(myself), 1, 0)
    pl.semaphore_wait(barrier, count)

    mine = rb.at[pl.ds(y * 4, 4)]
    slot = land.at[pl.ds(y * 4, 4), r % 4]

    def give(step):
        dz, dx, serves, myself = chip(step)
        cp = copy_to(
            mine, slot, gs.at[step], gd.at[((r % 4) // 2) * 4 + y], (dz * 8 + dx * 2 + core, goal)
        )
        return serves & jnp.logical_not(myself), cp

    for step in range(16):
        sends, cp = give(step)

        @pl.when(sends)
        def _():
            cp.start()

    @pl.when((goal == c) & (chip(0)[2]))
    def _():
        own = pltpu.make_async_copy(mine, slot, own_sem)
        own.start()
        own.wait()

    turn[...] = jnp.swapaxes(w_ref[...].reshape(32, 32, 128).astype(F32), 0, 1)
    for q in range(4):
        for e2 in range(2):
            at = q * 256 + e2 * 128
            tile = turn[e2 * 16 + q * 4 : e2 * 16 + q * 4 + 4].reshape(128, 128)
            wp_ref[at : at + 128] = tile.astype(BF16)
            wpt_ref[:, at : at + 128] = tile.T.astype(BF16)
    for b in range(8):
        lt[:, b * 128 : (b + 1) * 128] = left[b * 128 : (b + 1) * 128].T[:64].astype(BF16)

    bring.wait()

    def core_right(q):
        return copy_to(sr.at[1 - core, q], cr1.at[q], s1.at[q], r1.at[q], sibling)

    def x_right(q):
        return copy_to(tr1.at[q], cr2.at[x], s2.at[q], r2.at[x], (x_row(q), c))

    def pass_right(q):
        core_right(q).wait_recv()
        tr1[q] = (sr[core, q].astype(F32) + cr1[q].astype(F32)).astype(BF16)

        @pl.when(x != q)
        def _():
            x_right(q).start()

    @pl.loop(0, 4)
    def _(q):
        wq = wp_ref[pl.ds(pl.multiple_of(q * 256, 256), 256)]

        @pl.loop(0, 2, unroll=2)
        def _(b):
            g = g_ref[pl.ds(pl.multiple_of(b * 2048, 2048), 2048)]
            d = mm(wq, g, NT).astype(BF16)
            for e in range(8):
                for i in range(16):
                    dt[
                        pl.ds(pl.multiple_of(b * 512 + i * 32, 32), 32),
                        pl.ds(pl.multiple_of(q * 1024 + e * 128, 128), 128),
                    ] = d[e * 32 : e * 32 + 32, i * 128 : i * 128 + 128]

        gr = mm(lt[...], dt[:, pl.ds(pl.multiple_of(q * 1024, 1024), 1024)])
        for e1 in range(4):
            tile = jnp.concatenate(
                [gr[:, e1 * 128 : e1 * 128 + 128], gr[:, 512 + e1 * 128 : 640 + e1 * 128]], axis=0
            )
            turned = tile.T.astype(BF16)
            for kk in range(4):
                at = (e1 % 2) * 32
                sr[kk % 2, q, (kk // 2) * 2 + e1 // 2, at : at + 32] = turned[kk * 32 : kk * 32 + 32]
        core_right(q).start()

        @pl.when(q > 0)
        def _():
            pass_right(q - 1)

    def swap(q, m):
        there = land.at[pl.ds(q * 4, 4), core + 2 * m]
        return copy_to(there, there, ks.at[m * 4 + q], kd.at[m * 4 + q], sibling)

    for q in range(4):
        for m in range(2):
            row, col = giver(m, q)
            there = land.at[pl.ds(q * 4, 4), core + 2 * m]

            @unless((row == r) & (col == c))
            def _():
                copy_to(there, there, ks.at[m * 4 + q], gd.at[m * 4 + q], sibling).wait_recv()

            swap(q, m).start()
    pass_right(3)
    for q in range(4):
        for m in range(2):
            there = land.at[pl.ds(q * 4, 4), 1 - core + 2 * m]
            copy_to(there, there, ks.at[m * 4 + q], kd.at[m * 4 + q], sibling).wait_recv()

    bias[...] = jnp.zeros_like(bias)

    @pl.loop(0, 4, unroll=2)
    def _(b):
        rows = pl.ds(pl.multiple_of(b * 256, 256), 256)
        first = jnp.zeros((256, 128), F32)
        second = jnp.zeros((256, 128), F32)
        for q in range(4):
            part = land[q * 4 : q * 4 + 4].reshape(512, 128)
            first = first + mm(dt[rows, q * 1024 : q * 1024 + 512], part)
            second = second + mm(dt[rows, q * 1024 + 512 : q * 1024 + 1024], part)
        for m in range(4):
            even, odd = slice(m * 64, m * 64 + 32), slice(m * 64 + 32, m * 64 + 64)
            one = first[even] + pltpu.roll(second[even], 64, 1)
            two = second[odd] + pltpu.roll(first[odd], 64, 1)
            at = (m % 2) * 32
            glx[b * 2 + m // 2, at : at + 32] = (jnp.where(low32, one, two) * (1 / 64)).astype(BF16)
        g = g_ref[pl.ds(pl.multiple_of(b * 1024, 1024), 1024)]
        bias[...] += jnp.sum(g.astype(F32).reshape(64, 16, 128), 0)

    for n in range(8):
        glx[n, 64:80] = bias[...].astype(BF16)
    lefts = []
    for d in range(1, 8):
        cc = (c + d) % 8
        lefts.append(copy_to(glx.at[cc], cl.at[c], s5.at[d], r5.at[d], (r, cc)))
        lefts[-1].start()

    def core_map(q):
        return copy_to(sw.at[1 - core, q], cw1.at[q], s7.at[q], r7.at[q], sibling)

    def x_map(q):
        return copy_to(tw1.at[q], cw2.at[x], s8.at[q], r8.at[x], (x_row(q), c))

    def pass_map(q):
        core_map(q).wait_recv()
        tw1[q] = (sw[core, q].astype(F32) + cw1[q].astype(F32)).astype(BF16)

        @pl.when(x != q)
        def _():
            x_map(q).start()

    def z_right(d):
        zz = (z + d) % 4
        return copy_to(tr2.at[zz], cr3.at[d], s3.at[d], r3.at[d], (z_row(zz), c))

    def out_right(cc):
        return copy_to(tr3, fr.at[piece], s4.at[cc], r4.at[piece], (owner, cc))

    def out_left(d):
        return copy_to(tl, fl.at[c], s6.at[d], r6.at[d], (r, (c + d) % 8))

    @pl.loop(0, 4)
    def _(q):
        part = land[pl.ds(q * 4, 4)].reshape(512, 128)

        @pl.loop(0, 2, unroll=2)
        def _(b):
            rows = pl.ds(pl.multiple_of(b * 512, 512), 512)
            for e2, l in enumerate((la, lb)):
                o = mm(l[rows], part, NT).astype(BF16)
                for e1 in range(4):
                    for i in range(16):
                        ot[
                            pl.ds(pl.multiple_of(q * 256 + (e2 * 4 + e1) * 32, 32), 32),
                            pl.ds(pl.multiple_of(b * 2048 + i * 128, 128), 128),
                        ] = o[i * 32 : i * 32 + 32, e1 * 128 : e1 * 128 + 128]

        @pl.when(q == 1)
        def _():
            for d in range(1, 4):
                n = (x + d) % 4
                copy_to(cr2.at[n], cr2.at[n], s2.at[0], r2.at[n], sibling).wait_recv()
            for d in (1, 2, 3, 0):
                zz = (z + d) % 4
                total = tr1[x, zz].astype(F32)
                for n in range(1, 4):
                    total = total + cr2[(x + n) % 4, zz].astype(F32)
                tr2[zz] = total.astype(BF16)
                if d:
                    z_right(d).start()

        @pl.when(q == 3)
        def _():
            for cp in lefts:
                cp.wait_recv()
            cl[c] = glx[c]
            total = cl[0].astype(F32)
            for n in range(1, 8):
                total = total + cl[n].astype(F32)
            tl[...] = total[:64].astype(BF16)
            bias[...] = total[64:]
            for d in range(1, 8):
                out_left(d).start()

        @pl.when(q == 2)
        def _():
            for d in range(1, 4):
                z_right(d).wait_recv()
            total = tr2[z].astype(F32)
            for n in range(1, 4):
                total = total + cr3[n].astype(F32)
            tr3[...] = total.astype(BF16)
            for cc in range(8):

                @unless((owner == r) & (c == cc))
                def _():
                    out_right(cc).start()

            @pl.when(owner == r)
            def _():
                fr[piece] = tr3[...]

        gw = mm(ot[pl.ds(pl.multiple_of(q * 256, 256), 256)], g_ref[...])
        for cc in range(2):
            for zz in range(4):
                at = cc * 128 + zz * 32
                sw[cc, q, zz] = gw[at : at + 32].astype(BF16)
        core_map(q).start()

        @pl.when(q > 0)
        def _():
            pass_map(q - 1)

    def z_map(d):
        zz = (z + d) % 4
        return copy_to(tw2.at[zz], cw3.at[d], s9.at[d], r9.at[d], (z_row(zz), c))

    def col_map(d):
        return copy_to(cw4.at[c], cw4.at[c], s10.at[d], r10.at[d], (r, (c + d) % 8))

    offset = off_ref[...]

    @pl.loop(0, 4)
    def _(b):
        update = mm(wpt_ref[...], ot[:, pl.ds(pl.multiple_of(b * 1024, 1024), 1024)])
        for i in range(8):
            at = pl.multiple_of(b * 1024 + i * 128, 128)
            pu_ref[pl.ds(at, 128)] = (update[:, i * 128 : i * 128 + 128].T + offset).astype(BF16)

        @pl.when(b == 0)
        def _():
            pass_map(3)

    put = pltpu.make_async_copy(pu_ref, pu_hbm, pu_sem)
    put.start()

    for d in range(1, 4):
        n = (x + d) % 4
        copy_to(cw2.at[n], cw2.at[n], s8.at[0], r8.at[n], sibling).wait_recv()
    for d in (1, 2, 3, 0):
        zz = (z + d) % 4
        total = tw1[x, zz].astype(F32)
        for n in range(1, 4):
            total = total + cw2[(x + n) % 4, zz].astype(F32)
        tw2[zz] = total.astype(BF16)
        if d:
            z_map(d).start()

    for d in range(1, 8):
        out_left(d).wait_recv()
    fl[c] = tl[...]
    for d in range(1, 4):
        z_map(d).wait_recv()
    total = tw2[z].astype(F32)
    for n in range(1, 4):
        total = total + cw3[n].astype(F32)
    cw4[c] = total.astype(BF16)
    for d in range(1, 8):
        col_map(d).start()
    for n in range(8):

        @unless((source(n) == r) & (goal == c))
        def _():
            copy_to(fr.at[n], fr.at[n], s4.at[n], r4.at[n], sibling).wait_recv()

    closing[...] = jnp.swapaxes(fr[...].reshape(16, 32, 128).astype(F32), 0, 1)

    def pair_grads(m):
        even, odd = closing[2 * m], closing[2 * m + 1]
        return jnp.concatenate(
            [
                fl[m // 2, pl.ds(pl.multiple_of((m % 2) * 32, 32), 32)],
                jnp.where(low16, even, pltpu.roll(odd, 64, 1)).astype(BF16),
                jnp.where(low16, pltpu.roll(even, 64, 1), odd).astype(BF16),
            ],
            axis=0,
        )

    acc[...] = jnp.zeros_like(acc)

    @pl.loop(0, 16, unroll=4)
    def _(m):
        grads = pair_grads(m)
        normed = (st[pl.ds(m * 2, 2)].reshape(128, 256) * gain).astype(BF16)
        acc[...] += mm(grads, normed)
        grads_all[m] = grads

    for n in range(2):
        for h in range(2):
            at = h * 32
            fs[n, at : at + 32] = acc[n * 32 : n * 32 + 32, h * 128 : h * 128 + 128]
        fs[n, 64:80] = bias[...]
    half = copy_to(fs.at[1 - core], fc1, s11.at[0], r11.at[0], sibling)
    half.start()

    def bring_adj(n):
        return pltpu.make_async_copy(
            adj_ref.at[n], adj_hbm.at[:, pl.ds(n * 8, 8)], adj_sem.at[n]
        )

    def adjoint(n):
        @pl.loop(0, 4, unroll=2)
        def _(p):
            m = n * 4 + p
            standard = st[pl.ds(m * 2, 2)].reshape(128, 256)
            inverse = inv[pl.ds(m * 2, 2)].reshape(128, 1)
            scaled = mm(grads_all[m], wt_ref[...], TN) * gain
            mean = jnp.mean(scaled, -1, keepdims=True)
            along = jnp.mean(scaled * standard, -1, keepdims=True)
            adj = inverse * (scaled - mean - standard * along)
            tall[pl.ds(p * 2, 2)] = adj.reshape(2, 64, 256)

        @pl.loop(0, 8, unroll=4)
        def _(b):
            rows = pl.ds(pl.multiple_of(b * 8, 8), 8)
            adj_ref[n, rows] = jnp.swapaxes(tall[:, rows], 0, 1)

        bring_adj(n).start()

    adjoint(0)
    half.wait_recv()
    fx[x] = (fs[core] + fc1[...]).astype(BF16)
    fxs = [
        copy_to(fx.at[x], fx.at[x], s13.at[d], r13.at[d], (x_row((x + d) % 4), c)) for d in range(1, 4)
    ]
    for cp in fxs:
        cp.start()
    adjoint(1)
    adjoint(2)
    for d in range(1, 8):
        col_map(d).wait_recv()
    total = cw4[0].astype(F32)
    for n in range(1, 8):
        total = total + cw4[n].astype(F32)
    wz[z] = total.astype(BF16)
    zs = [
        copy_to(wz.at[z], wz.at[z], s12.at[d], r12.at[d], (z_row((z + d) % 4), c)) for d in range(1, 4)
    ]
    for cp in zs:
        cp.start()
    for cp in fxs:
        cp.wait_recv()
    total = fx[0].astype(F32)
    for n in range(1, 4):
        total = total + fx[n].astype(F32)
    fz[z] = total.astype(BF16)
    fzs = [
        copy_to(fz.at[z], fz.at[z], s15.at[d], r15.at[d], (z_row((z + d) % 4), c)) for d in range(1, 4)
    ]
    for cp in fzs:
        cp.start()
    adjoint(3)
    for cp in zs:
        cp.wait_recv()
    wx[x] = wz[...]
    xs_ = [
        copy_to(wx.at[x], wx.at[x], s14.at[d], r14.at[d], (x_row((x + d) % 4), c)) for d in range(1, 4)
    ]
    for cp in xs_:
        cp.start()
    for cp in fzs:
        cp.wait_recv()
    total = fz[0].astype(F32)
    for n in range(1, 4):
        total = total + fz[n].astype(F32)
    ff[core] = total[:64]
    end = copy_to(ff.at[core], ff.at[core], s11.at[1], r11.at[1], sibling)
    end.start()
    bias_ref[...] = jnp.sum(total[64:], 0, keepdims=True)
    end.wait_recv()
    for n in range(2):
        for h in range(2):
            fac_ref[n, :, h * 128 : h * 128 + 128] = ff[n, h * 32 : h * 32 + 32]
    for cp in xs_:
        cp.wait_recv()
    last = copy_to(wx, wc, s16.at[0], r16.at[0], sibling)
    last.start()

    def spread(e2, parts):
        map_ref[:, pl.ds(pl.multiple_of(e2 * 16, 16), 16)] = jnp.swapaxes(
            parts.reshape(16, 32, 128).astype(F32), 0, 1
        )

    spread(core, wx[...])
    last.wait_recv()
    spread(1 - core, wc[...])

    for step in range(16):
        sends, cp = give(step)

        @pl.when(sends)
        def _():
            cp.wait_send()

    for q in range(4):
        core_right(q).wait_send()
        core_map(q).wait_send()

        @pl.when(x != q)
        def _():
            x_right(q).wait_send()
            x_map(q).wait_send()

        for m in range(2):
            swap(q, m).wait_send()
    for d in range(1, 4):
        z_right(d).wait_send()
        z_map(d).wait_send()
    for d in range(1, 8):
        out_left(d).wait_send()
        col_map(d).wait_send()
    for cc in range(8):

        @unless((owner == r) & (c == cc))
        def _():
            out_right(cc).wait_send()

    put.wait()
    for n in range(4):
        bring_adj(n).wait()
    for cp in lefts + zs + fxs + xs_ + fzs + [half, last, end]:
        cp.wait_send()


def run(x, gain, w1, w2, g, w, off):
    vm = pl.BlockSpec(memory_space=pltpu.VMEM)
    anywhere = pl.BlockSpec(memory_space=pl.ANY)

    def b16(*shape):
        return pltpu.VMEM(shape, BF16)

    def f32(*shape):
        return pltpu.VMEM(shape, F32)

    sems = []
    for n in (4, 4, 4, 8, 8, 8, 4, 4, 4, 8, 2, 4, 4, 4, 4, 1):
        sems += [pltpu.SemaphoreType.DMA((n,)), pltpu.SemaphoreType.DMA((n,))]
    return pl.pallas_call(
        kernel,
        out_shape=(
            jax.ShapeDtypeStruct((4096, 128), BF16),
            jax.ShapeDtypeStruct((64, 32, 256), F32),
            jax.ShapeDtypeStruct((2, 32, 256), F32),
            jax.ShapeDtypeStruct((1, 128), F32),
            jax.ShapeDtypeStruct((32, 32, 128), F32),
        ),
        in_specs=[vm, vm, vm, vm, anywhere, vm, vm],
        out_specs=(anywhere, anywhere, vm, vm, vm),
        scratch_shapes=[
            f32(32, 64, 256), f32(32, 64, 1), b16(4096, 128), b16(64, 256), b16(1024, 128), b16(128, 1024),
            b16(4096, 128), f32(32, 32, 128), f32(4, 64, 8, 256),
            b16(1024, 128), b16(1024, 128), b16(64, 1024), f32(1024, 128), f32(32, 16, 128),
            b16(16, 32, 128), b16(16, 4, 32, 128), b16(1024, 4096), b16(1024, 4096), b16(8, 80, 128),
            b16(2, 4, 4, 64, 128), b16(4, 4, 64, 128), b16(4, 4, 64, 128), b16(4, 4, 64, 128),
            b16(4, 64, 128), b16(4, 64, 128), b16(64, 128), b16(8, 64, 128),
            b16(2, 4, 4, 32, 128), b16(4, 4, 32, 128), b16(4, 4, 32, 128), b16(4, 4, 32, 128),
            b16(4, 32, 128), b16(4, 32, 128), b16(8, 32, 128), b16(4, 32, 128), b16(4, 4, 32, 128),
            b16(4, 4, 32, 128),
            b16(8, 80, 128), b16(64, 128), b16(8, 64, 128), f32(16, 128), f32(32, 16, 128), f32(64, 256),
            b16(16, 64, 128), f32(8, 64, 256), f32(2, 80, 128), f32(80, 128), b16(4, 80, 128), b16(4, 80, 128), f32(2, 64, 128),
            pltpu.SemaphoreType.DMA((16,)), pltpu.SemaphoreType.DMA((8,)),
            pltpu.SemaphoreType.DMA((8,)), pltpu.SemaphoreType.DMA((8,)), pltpu.SemaphoreType.DMA,
            pltpu.SemaphoreType.DMA, pltpu.SemaphoreType.DMA, pltpu.SemaphoreType.DMA((4,)),
            *sems,
        ],
        compiler_params=pltpu.CompilerParams(
            collective_id=0, has_side_effects=True, vmem_limit_bytes=56 << 20
        ),
        name="outer_product_mean",
    )(x, gain, w1, w2, g, w, off)


def hand_over_kernel(*refs):
    sources, goals, sem = refs[:5], refs[5:10], refs[10]
    copies = []
    for source, goal, parts in zip(sources, goals, (4, 8, 1, 1, 1)):
        rows = source.shape[0] // parts
        for n in range(parts):
            at = pl.ds(n * rows, rows)
            copies.append((source.at[at], goal.at[at]))
    copies = [pltpu.make_async_copy(a, b, sem.at[n]) for n, (a, b) in enumerate(copies)]
    for cp in copies:
        cp.start()
    for cp in copies:
        cp.wait()


def hand_over(*arrays):
    anywhere = pl.BlockSpec(memory_space=pl.ANY)
    return pl.pallas_call(
        hand_over_kernel,
        out_shape=tuple(jax.ShapeDtypeStruct(a.shape, a.dtype) for a in arrays),
        in_specs=[pl.BlockSpec(memory_space=pltpu.VMEM)] * 5,
        out_specs=(anywhere,) * 5,
        scratch_shapes=[pltpu.SemaphoreType.DMA((15,))],
        compiler_params=pltpu.CompilerParams(vmem_limit_bytes=62 << 20),
        name="hand_over",
    )(*arrays)


def per_device(
    sequence_stack,
    feature_multiplier,
    first_factor_map,
    second_factor_map,
    emitted_map,
    emitted_offset,
    upstream_adjoint,
):
    pu, adj, fac, bias, w = run(
        sequence_stack,
        feature_multiplier.reshape(1, 256),
        first_factor_map.T,
        second_factor_map.T,
        upstream_adjoint.reshape(4096, 128),
        emitted_map,
        emitted_offset.reshape(1, 128),
    )
    pu, adj, fac, bias, w = hand_over(pu, adj, fac, bias, w)
    return (
        pu.reshape(32, 128, 128),
        adj,
        fac.transpose(0, 2, 1),
        w.reshape(1024, 128),
        bias.reshape(128),
    )


def solution(mesh):
    return jax.shard_map(
        per_device,
        mesh=mesh,
        in_specs=(P(None, "row", None), P(), P(), P(), P(), P(), P("row", "col", None)),
        out_specs=(P("row", "col", None), P(None, "row", None), P(), P(), P()),
        check_vma=False,
    )
```
